256 devices in a mesh: state: 16 (over y, z_lo), tile: 16 (over z_hi, x, core).
Axes of the slice: x: 4, y: 4, z: 8 (z_hi: 2, z_lo: 4; z = z_hi * 4 + z_lo), core: 2. Of those that a mesh axis runs over, the one named last changes fastest.
Arguments:
- pair_tiles: bfloat16 [16, 16, 32, 32, 128], P('state', 'tile'), may hold values from -60 to 60
- targets: int32 [16, 16, 2, 4, 128], P('state', 'tile'), may hold values from 0 to 63, as said below
- offsets: int32 [16], replicated, may hold values from 0 to 128, as said below
- ln_gain: float32 [128], replicated, may hold values from 0.5 to 1.5
- ln_bias: float32 [128], replicated, may hold values from -3 to 3
- w_query: bfloat16 [128, 128], replicated, may hold values from -0.5 to 0.5
- w_key: bfloat16 [128, 128], replicated, may hold values from -0.5 to 0.5
- w_value: bfloat16 [128, 128], replicated, may hold values from -0.5 to 0.5
- w_pairbias: float32 [128, 4], replicated, may hold values from -25 to 25
- w_gate: bfloat16 [128, 128], replicated, may hold values from -0.5 to 0.5
- gate_bias: float32 [128], replicated, may hold values from -4 to 4
- w_output: bfloat16 [128, 128], replicated, may hold values from -0.5 to 0.5
- out_bias: float32 [128], replicated, may hold values from -3 to 3
- w_distogram: float32 [128, 64], replicated, may hold values from -4 to 4
- dist_bias: float32 [64], replicated, may hold values from -4 to 4
Outputs:
- shared_grad: float32 [8, 16, 2, 2, 128, 128], P(None, 'tile', None, None, 'state')
The draws below stay inside these ranges and needn't reach their ends.
Inputs may be any that keep to these rules, and one draw needn't show every extreme that they name: `targets`: symmetric: the bin of crop pair (x, y) equals that of (y, x) in every state. `offsets`: each is a multiple of 32; some state starts at 0 and some state at 128.
All inputs are finite; a program needn't handle non-finite values.
Results may differ from the reference program's by a relative error of at most 0.015.
Values may be sent and summed in bfloat16 or wider, within the bound.
A program may use at most 64 MiB of HBM per device.

```python
import math
import jax
import jax.numpy as jnp
from jax import lax

C = 128
H = 4
HD = 32
NB = 64
L = 128
STATES = 16
NT = 16
TG = 4
B = 32
RA = 2
LFULL = 256
UT = 8


def draw_pair_tiles(key, part):
    base_key = jax.random.fold_in(key, 11)
    full_shape = (STATES, L, L, C)
    pair_field = jnp.clip(jax.random.normal(base_key, full_shape, jnp.float32), -6.0, 6.0)
    tiled = pair_field.reshape(STATES, TG, B, TG, B, C).transpose(0, 1, 3, 2, 4, 5).reshape(STATES, NT, B, B, C)
    return tiled.astype(jnp.bfloat16)


def draw_targets(key, part):
    raw_bins = jax.random.randint(jax.random.fold_in(key, 21), (STATES, L, L), 0, NB)
    index = jnp.arange(L, dtype=jnp.int32)
    upper_mask = (index[:, None] <= index[None, :])[None]
    symmetric = jnp.where(upper_mask, raw_bins, jnp.swapaxes(raw_bins, 1, 2))
    return symmetric.reshape(STATES, TG, NT, RA, L).transpose(0, 2, 3, 1, 4).astype(jnp.int32)


def draw_offsets(key, part):
    steps_drawn = jax.random.randint(jax.random.fold_in(key, 31), (STATES,), 0, TG + 1)
    top_state = jax.random.randint(jax.random.fold_in(key, 32), (), 0, STATES)
    bottom_state = (top_state + 1 + jax.random.randint(jax.random.fold_in(key, 33), (), 0, STATES - 1)) % STATES
    index = jnp.arange(STATES, dtype=jnp.int32)
    chosen = jnp.where(index == top_state, TG, jnp.where(index == bottom_state, 0, steps_drawn))
    return (B * chosen).astype(jnp.int32)


def draw_w_pairbias(key, part):
    base_key = jax.random.fold_in(key, 41)
    matrix = jnp.clip(jax.random.normal(base_key, (C, H), jnp.float32), -6.0, 6.0) / math.sqrt(C)
    return matrix.astype(jnp.float32)


def draw_w_distogram(key, part):
    base_key = jax.random.fold_in(key, 51)
    matrix = jnp.clip(jax.random.normal(base_key, (C, NB), jnp.float32), -6.0, 6.0) / math.sqrt(C)
    return matrix.astype(jnp.float32)


def noise(own_key, shape, spread, limit, kind=jnp.bfloat16):
    values = spread * jax.random.normal(own_key, shape, jnp.float32)
    return jnp.clip(values, min=-limit, max=limit).astype(kind)


def setup_inputs(seed: int = 0) -> dict:
    splits = jax.random.split(jax.random.key(seed), 16)
    pair_tiles = draw_pair_tiles(jax.random.fold_in(splits[15], 71), 0)
    targets = draw_targets(jax.random.fold_in(splits[15], 71), 0)
    offsets = draw_offsets(jax.random.fold_in(splits[15], 71), 0)
    ln_gain = jnp.clip(1.0 + 0.1 * jax.random.normal(splits[3], (C,), jnp.float32), 0.5, 1.5)
    ln_bias = noise(splits[4], (C,), 0.5, 3.0, jnp.float32)
    w_query = noise(splits[5], (C, H * HD), C ** -0.5, 0.5)
    w_key = noise(splits[6], (C, H * HD), C ** -0.5, 0.5)
    w_value = noise(splits[7], (C, H * HD), C ** -0.5, 0.5)
    w_pairbias = draw_w_pairbias(jax.random.fold_in(splits[15], 71), 0)
    w_gate = noise(splits[9], (C, H * HD), C ** -0.5, 0.5)
    gate_bias = noise(splits[10], (H * HD,), 1.0, 4.0, jnp.float32)
    w_output = noise(splits[11], (H * HD, C), (H * HD) ** -0.5, 0.5)
    out_bias = noise(splits[12], (C,), 0.5, 3.0, jnp.float32)
    w_distogram = draw_w_distogram(jax.random.fold_in(splits[15], 71), 0)
    dist_bias = noise(splits[14], (NB,), 1.0, 4.0, jnp.float32)
    return dict(pair_tiles=pair_tiles, targets=targets, offsets=offsets, ln_gain=ln_gain, ln_bias=ln_bias, w_query=w_query, w_key=w_key, w_value=w_value, w_pairbias=w_pairbias, w_gate=w_gate, gate_bias=gate_bias, w_output=w_output, out_bias=out_bias, w_distogram=w_distogram, dist_bias=dist_bias)


def layer_norm(pair_field, ln_gain, ln_bias):
    center = pair_field - lax.optimization_barrier(jnp.mean(pair_field, axis=-1, keepdims=True))
    inverse = lax.rsqrt(lax.optimization_barrier(jnp.mean(center * center, axis=-1, keepdims=True)) + 1e-05)
    normed = center * inverse
    return (normed * ln_gain + ln_bias, normed, inverse)

def product(left_op, right_op, form):
    return jnp.einsum(form, left_op.astype(jnp.float32), right_op.astype(jnp.float32), precision=lax.Precision.HIGHEST)

def probabilities(queries, key_proj, bias_full):
    scores = product(queries, key_proj, 'rjhd,rkhd->rhjk')
    scores = scores * (1.0 / math.sqrt(HD)) + bias_full[None]
    row_max = lax.optimization_barrier(jnp.max(scores, axis=-1, keepdims=True))
    exp_scores = jnp.exp(scores - row_max)
    return exp_scores / lax.optimization_barrier(jnp.sum(exp_scores, axis=-1, keepdims=True))

def reference(pair_tiles, targets, offsets, ln_gain, ln_bias, w_query, w_key, w_value, w_pairbias, w_gate, gate_bias, w_output, out_bias, w_distogram, dist_bias):
    hidden_width = H * HD
    block_rows = 8
    groups = L // block_rows
    inv_root = 1.0 / math.sqrt(HD)

    def split_rows(values_in):
        return values_in.reshape((groups, block_rows) + values_in.shape[1:])

    def state_gradient(tiled, target_rows):
        pair_field = tiled.reshape(TG, TG, B, B, C).transpose(0, 2, 1, 3, 4).reshape(L, L, C).astype(jnp.float32)
        target = target_rows.transpose(2, 0, 1, 3).reshape(L, L)
        normed_out, normed, inverse = layer_norm(pair_field, ln_gain, ln_bias)
        flat_b = normed_out.astype(jnp.bfloat16).reshape(L * L, C)

        def project(weight):
            return jnp.dot(flat_b, weight, preferred_element_type=jnp.float32).astype(jnp.bfloat16).reshape(L, L, H, HD)
        queries = project(w_query)
        key_proj = project(w_key)
        value_proj = project(w_value)
        gate_act = jax.nn.sigmoid(jnp.dot(flat_b, w_gate, preferred_element_type=jnp.float32) + gate_bias).reshape(L, L, hidden_width)
        bias_full = product(normed_out, w_pairbias, 'jkc,ch->hjk')

        def forward_block(block_args):
            query_blk, key_blk, value_blk = block_args
            weights_b = probabilities(query_blk, key_blk, bias_full).astype(jnp.bfloat16)
            return product(weights_b, value_blk, 'rhjk,rkhd->rjhd')
        attended = lax.map(forward_block, (split_rows(queries), split_rows(key_proj), split_rows(value_proj))).reshape(L, L, hidden_width)
        gated_out = (gate_act * attended).astype(jnp.bfloat16)
        updated = pair_field + jnp.dot(gated_out.reshape(L * L, hidden_width), w_output, preferred_element_type=jnp.float32).reshape(L, L, C) + out_bias
        logits = product(updated + jnp.swapaxes(updated, 0, 1), w_distogram, 'xyc,cb->xyb') + dist_bias
        row_max = lax.optimization_barrier(jnp.max(logits, axis=-1, keepdims=True))
        exp_logits = jnp.exp(logits - row_max)
        bin_prob = exp_logits / lax.optimization_barrier(jnp.sum(exp_logits, axis=-1, keepdims=True))
        onehot = (target[:, :, None] == jnp.arange(NB, dtype=jnp.int32)[None, None, :]).astype(jnp.float32)
        residual_grad = bin_prob - onehot
        logit_grad = residual_grad + jnp.swapaxes(residual_grad, 0, 1)
        pair_grad = product(logit_grad, w_distogram, 'xyb,cb->xyc')
        out_grad = product(pair_grad.astype(jnp.bfloat16), w_output, 'xyc,wc->xyw')
        att_grad_b = (out_grad * gate_act).astype(jnp.bfloat16).reshape(L, L, H, HD)
        gate_grad = out_grad * attended * gate_act * (1.0 - gate_act)

        def backward_block(bias_sum, block_args):
            query_blk, key_blk, value_blk, grad_blk = block_args
            attn_prob = probabilities(query_blk, key_blk, bias_full)
            weights_b = attn_prob.astype(jnp.bfloat16)
            value_grad = product(weights_b, grad_blk, 'rhjk,rjhd->rkhd')
            weight_grad = product(grad_blk, value_blk, 'rjhd,rkhd->rhjk')
            score_grad = attn_prob * (weight_grad - lax.optimization_barrier(jnp.sum(attn_prob * weight_grad, axis=-1, keepdims=True)))
            score_b = score_grad.astype(jnp.bfloat16)
            query_grad = product(score_b, key_blk, 'rhjk,rkhd->rjhd') * inv_root
            key_grad = product(score_b, query_blk, 'rhjk,rjhd->rkhd') * inv_root
            return (bias_sum + lax.optimization_barrier(jnp.sum(score_grad, axis=0)), (query_grad, key_grad, value_grad))
        bias_grad, grad_parts = lax.scan(backward_block, jnp.zeros((H, L, L), jnp.float32), (split_rows(queries), split_rows(key_proj), split_rows(value_proj), split_rows(att_grad_b)))
        query_grad, key_grad, value_grad = grad_parts

        def back_project(grad_part, weight):
            return product(grad_part.reshape(L, L, hidden_width).astype(jnp.bfloat16), weight, 'xyw,cw->xyc')
        normed_grad = back_project(query_grad, w_query) + back_project(key_grad, w_key) + back_project(value_grad, w_value) + back_project(gate_grad, w_gate)
        normed_grad = normed_grad + product(bias_grad, w_pairbias, 'hjk,ch->jkc')
        scaled = normed_grad * ln_gain
        ln_back = inverse * (scaled - lax.optimization_barrier(jnp.mean(scaled, axis=-1, keepdims=True)) - normed * lax.optimization_barrier(jnp.mean(scaled * normed, axis=-1, keepdims=True)))
        return (pair_grad + ln_back).astype(jnp.bfloat16)

    def accumulate(accum, state_args):
        tiled, target_rows, offset = state_args
        grad_state = state_gradient(tiled, target_rows).astype(jnp.float32)
        row_start = offset.astype(jnp.int32)
        zero_index = jnp.zeros((), jnp.int32)
        window = lax.dynamic_slice(accum, (row_start, row_start, zero_index), (L, L, C))
        accum = lax.dynamic_update_slice(accum, window + grad_state, (row_start, row_start, zero_index))
        return (accum, None)
    accum, _ = lax.scan(accumulate, jnp.zeros((LFULL, LFULL, C), jnp.float32), (pair_tiles, targets, offsets))
    return accum.reshape(UT, NT, RA, 2, L, C)
```

```python
import math

import jax
import jax.numpy as jnp
from jax import lax
from jax.experimental import pallas as pl
from jax.experimental.pallas import tpu as pltpu
from jax.sharding import PartitionSpec as P

C = 128
H = 4
HD = 32
NB = 64
L = 128
S = 16
T = 16
R = 8
F32 = jnp.float32
BF16 = jnp.bfloat16
I32 = jnp.int32
MESH = pl.DeviceIdType.MESH
LOG2E = 1.0 / math.log(2.0)
INV_ROOT = 1.0 / math.sqrt(HD)

SCRATCH = dict(
    gain_v=pltpu.VMEM((1, C), F32),
    lbias_v=pltpu.VMEM((1, C), F32),
    wq_v=pltpu.VMEM((C, C), BF16),
    wk_v=pltpu.VMEM((C, C), BF16),
    wv_v=pltpu.VMEM((C, C), BF16),
    wg_v=pltpu.VMEM((C, C), BF16),
    wo_v=pltpu.VMEM((C, C), BF16),
    wpb_v=pltpu.VMEM((C, H), F32),
    gbias_v=pltpu.VMEM((1, C), F32),
    obias_v=pltpu.VMEM((1, C), F32),
    wd_v=pltpu.VMEM((C, NB), F32),
    dbias_v=pltpu.VMEM((1, NB), F32),
    targets_v=pltpu.VMEM((2, 4, L), I32),
    w_sem=pltpu.SemaphoreType.DMA((13,)),
    eye=pltpu.VMEM((C, C), BF16),
    hmask=pltpu.VMEM((H, C, C), BF16),
    shift=pltpu.VMEM((L, L), BF16),
    spread=pltpu.VMEM((256, S * 64), BF16),
    w_in_t=pltpu.VMEM((4 * C, C), BF16),
    w_in=pltpu.VMEM((C, 4 * C), BF16),
    wo_t=pltpu.VMEM((C, C), BF16),
    wd_t3=pltpu.VMEM((NB, 3 * C), BF16),
    wd3=pltpu.VMEM((C, 3 * NB), BF16),
    gain_b=pltpu.VMEM((C, L), F32),
    lbias_b=pltpu.VMEM((C, L), F32),
    gbias_b=pltpu.VMEM((C, L), F32),
    obias_b=pltpu.VMEM((C, L), F32),
    dbias_b=pltpu.VMEM((NB, L), F32),
    wpb_b=pltpu.VMEM((H, C, L), F32),
    zb=pltpu.VMEM((R, L, C), BF16),
    zt=pltpu.VMEM((R, C, L), F32),
    xh=pltpu.VMEM((R, C, L), F32),
    inv=pltpu.VMEM((R, 1, L), F32),
    znb=pltpu.VMEM((R, C, L), BF16),
    qt=pltpu.VMEM((R, C, L), BF16),
    kt=pltpu.VMEM((R, C, L), BF16),
    vt=pltpu.VMEM((R, C, L), BF16),
    vn=pltpu.VMEM((R, L, C), BF16),
    gt=pltpu.VMEM((R, C, L), F32),
    ot=pltpu.VMEM((R, C, L), F32),
    at=pltpu.VMEM((R, H, L, L), F32),
    bias_t=pltpu.VMEM((H, L, L), F32),
    lgt=pltpu.VMEM((R, NB, L), F32),
    lgn=pltpu.VMEM((R * L, C), F32),
    mirror=pltpu.VMEM((R, NB, L), F32),
    dp=pltpu.VMEM((R, C, L), F32),
    d4=pltpu.VMEM((R, 4 * C, L), BF16),
    dbt=pltpu.VMEM((H, L, L), F32),
    dbs=pltpu.VMEM((H * R, L), F32),
    grad=pltpu.VMEM((R, L, C), F32),
    tg_stage=pltpu.VMEM((4, 8, L), I32),
    tg_recv=pltpu.VMEM((4, 8, L), I32),
    b_stage=pltpu.VMEM((H * R, L), F32),
    b_recv=pltpu.VMEM((T, H * R, L), F32),
    c_stage=pltpu.VMEM((T, 32, L), BF16),
    c_recv=pltpu.VMEM((T, 32, L), BF16),
    e_stage=pltpu.VMEM((T, 32, L), BF16),
    e_recv=pltpu.VMEM((T, 32, L), BF16),
    f_stage=pltpu.VMEM((4, S, 16, C), BF16),
    f_recv=pltpu.VMEM((S, 4, 16, C), BF16),
    a_send=pltpu.SemaphoreType.DMA((4,)),
    a_sem=pltpu.SemaphoreType.DMA,
    tg_send=pltpu.SemaphoreType.DMA((4,)),
    tg_sem=pltpu.SemaphoreType.DMA,
    b_send=pltpu.SemaphoreType.DMA((16,)),
    b_sem=pltpu.SemaphoreType.DMA((3,)),
    c_send=pltpu.SemaphoreType.DMA((T,)),
    c_sem=pltpu.SemaphoreType.DMA,
    e_send=pltpu.SemaphoreType.DMA((T,)),
    e_sem=pltpu.SemaphoreType.DMA,
    f_send=pltpu.SemaphoreType.DMA((4, S)),
    f_sem=pltpu.SemaphoreType.DMA,
)
NAMES = tuple(SCRATCH)


class Refs:
    pass


def dot(left, right):
    return jnp.dot(left, right, preferred_element_type=F32)


def dot_nt(left, right):
    return lax.dot_general(left, right, (((1,), (1,)), ((), ())), preferred_element_type=F32)


def halves(values):
    high = values.astype(BF16)
    low = (values - high.astype(F32)).astype(BF16)
    return high, low


def three(values):
    high, low = halves(values)
    return jnp.concatenate([high, low, high], axis=0)


def total(values):
    return jnp.sum(values, axis=0, keepdims=True)


def column(row):
    width = row.shape[1]
    return jnp.transpose(jnp.broadcast_to(row, (L, width)))


def kernel(
    tiles,
    targets,
    offsets,
    gain,
    lbias,
    wq,
    wk,
    wv,
    wpb,
    wg,
    gbias,
    wo,
    obias,
    wd,
    dbias,
    out,
    *scratch,
):
    m = Refs()
    for name, ref in zip(NAMES, scratch):
        setattr(m, name, ref)
    state = lax.axis_index("state")
    tile = lax.axis_index("tile")
    band = tile // 4
    sub = tile % 4

    barrier = pltpu.get_barrier_semaphore()

    def greet_tile(step, carry):
        peer = lax.rem(tile + step, T)
        pl.semaphore_signal(barrier, inc=1, device_id=(state, peer), device_id_type=MESH)
        return carry

    lax.fori_loop(1, T, greet_tile, 0)

    def greet_state(step, carry):
        peer = lax.rem(state + step, S)
        for group in range(4):
            pl.semaphore_signal(
                barrier, inc=1, device_id=(peer, 4 * group + band), device_id_type=MESH
            )
        return carry

    lax.fori_loop(1, S, greet_state, 0)

    loads = []
    for index, (source, target) in enumerate(
        [
            (gain, m.gain_v),
            (lbias, m.lbias_v),
            (wq, m.wq_v),
            (wk, m.wk_v),
            (wv, m.wv_v),
            (wg, m.wg_v),
            (wo, m.wo_v),
            (wpb, m.wpb_v),
            (gbias, m.gbias_v),
            (obias, m.obias_v),
            (wd, m.wd_v),
            (dbias, m.dbias_v),
            (targets.at[0, 0], m.targets_v),
        ]
    ):
        load = pltpu.make_async_copy(source, target, m.w_sem.at[index])
        load.start()
        loads.append(load)

    rows_i = lax.broadcasted_iota(I32, (C, C), 0)
    cols_i = lax.broadcasted_iota(I32, (C, C), 1)
    m.eye[...] = jnp.where(rows_i == cols_i, 1.0, 0.0).astype(BF16)
    for head in range(H):
        m.hmask[head] = jnp.where(cols_i // HD == head, 1.0, 0.0).astype(BF16)
    m.shift[...] = jnp.where(((rows_i - offsets[state] + L) & (L - 1)) == cols_i, 1.0, 0.0).astype(BF16)
    rows_o = lax.broadcasted_iota(I32, (256, L), 0)
    cols_o = lax.broadcasted_iota(I32, (256, L), 1)
    row_in = 8 * ((rows_o >> 4) & 1) + (rows_o & 7)
    same_row = row_in == (cols_o & 15)
    band_gap = 32 * ((rows_o >> 5) - ((cols_o >> 4) & 3))
    upper_half = (rows_o >> 3) & 1
    for index in range(S // 2):
        offset = jnp.where(cols_o < 64, offsets[2 * index], offsets[2 * index + 1])
        wrapped = jnp.where(offset > 8 * state, 1, 0)
        chosen = same_row & (band_gap == offset) & (upper_half == wrapped)
        m.spread[:, L * index : L * (index + 1)] = jnp.where(chosen, 1.0, 0.0).astype(BF16)
    for load in loads:
        load.wait()
    for group in range(4):
        m.tg_stage[group] = jnp.concatenate([m.targets_v[:, group, :]] * 4, axis=0)

    pl.semaphore_wait(barrier, T - 1 + 4 * (S - 1))

    def tile_copy(step):
        other = lax.rem(sub + step, 4)
        return pltpu.make_async_remote_copy(
            src_ref=tiles.at[0, 0, pl.ds(R * other, R)],
            dst_ref=m.zb.at[:, pl.ds(pl.multiple_of(32 * sub, 32), 32), :],
            send_sem=m.a_send.at[step],
            recv_sem=m.a_sem,
            device_id=(state, 4 * band + other),
            device_id_type=MESH,
        )

    for step in (2, 3, 1):
        tile_copy(step).start()
    pltpu.make_async_copy(
        tiles.at[0, 0, pl.ds(R * sub, R)],
        m.zb.at[:, pl.ds(pl.multiple_of(32 * sub, 32), 32), :],
        m.a_sem,
    ).start()
    for group in range(4):
        dest = 4 * group + band

        @pl.when(dest != tile)
        def _():
            pltpu.make_async_remote_copy(
                src_ref=m.tg_stage.at[group],
                dst_ref=m.tg_recv.at[sub],
                send_sem=m.tg_send.at[group],
                recv_sem=m.tg_sem,
                device_id=(state, dest),
                device_id_type=MESH,
            ).start()

        @pl.when(dest == tile)
        def _():
            pltpu.make_async_copy(m.tg_stage.at[group], m.tg_recv.at[sub], m.tg_sem).start()

    eye = m.eye[...]
    for index, ref in enumerate((m.wq_v, m.wk_v, m.wv_v, m.wg_v)):
        weight = ref[...]
        m.w_in[:, C * index : C * (index + 1)] = weight
        m.w_in_t[C * index : C * (index + 1), :] = dot_nt(eye, weight).astype(BF16)
    m.wo_t[...] = dot_nt(eye, m.wo_v[...]).astype(BF16)
    head_w = m.wd_v[...]
    high, low = halves(2.0 * head_w)
    m.wd3[...] = jnp.concatenate([high, high, low], axis=1)
    centred = head_w - jnp.mean(head_w, axis=1, keepdims=True)
    high, low = halves(jnp.transpose(centred))
    m.wd_t3[...] = jnp.concatenate([high, high, low], axis=1)
    m.gain_b[...] = column(m.gain_v[...])
    m.lbias_b[...] = column(m.lbias_v[...])
    m.gbias_b[...] = column(m.gbias_v[...])
    m.obias_b[...] = column(m.obias_v[...])
    m.dbias_b[...] = column(m.dbias_v[...])
    for head in range(H):
        m.wpb_b[head] = jnp.broadcast_to(m.wpb_v[:, head : head + 1], (C, L))
    m.dbt[...] = jnp.zeros_like(m.dbt)

    pltpu.make_async_copy(m.zb, m.zb, m.a_sem).wait()

    def norm_row(row, carry):
        z = dot_nt(m.eye[...], m.zb[row])
        centre = z - total(z) * (1.0 / C)
        inverse = lax.rsqrt(total(centre * centre) * (1.0 / C) + 1e-05)
        normed = centre * inverse
        zn = normed * m.gain_b[...] + m.lbias_b[...]
        m.zt[row] = z
        m.xh[row] = normed
        m.inv[row] = inverse
        m.znb[row] = zn.astype(BF16)
        for head in range(H):
            m.b_stage[pl.ds(R * head + row, 1), :] = total(zn * m.wpb_b[head])
        return carry

    lax.fori_loop(0, R, norm_row, 0)

    half = tile // 8
    place = tile % 8
    partner = 8 * (1 - half) + place

    def bias_copy(source, slot, index, sem, dest):
        return pltpu.make_async_remote_copy(
            src_ref=source,
            dst_ref=m.b_recv.at[slot],
            send_sem=m.b_send.at[index],
            recv_sem=m.b_sem.at[sem],
            device_id=(state, dest),
            device_id_type=MESH,
        )

    bias_copy(m.b_stage, tile, 0, 0, partner).start()
    for step in range(1, 8):
        dest = 8 * half + (place + step) % 8
        bias_copy(m.b_stage, tile, step, 1, dest).start()
    pltpu.make_async_copy(m.b_stage, m.b_recv.at[tile], m.b_sem.at[1]).start()

    def project_row(row, carry):
        proj = dot(m.w_in_t[...], m.znb[row])
        keys = proj[C : 2 * C].astype(BF16)
        values = proj[2 * C : 3 * C].astype(BF16)
        queries = proj[:C].astype(BF16)
        m.qt[row] = queries
        m.kt[row] = keys
        m.vt[row] = values
        m.gt[row] = jax.nn.sigmoid(proj[3 * C :] + m.gbias_b[...])
        keys_n = dot_nt(m.eye[...], keys).astype(BF16)
        m.vn[row] = dot_nt(m.eye[...], values).astype(BF16)
        stacked = jnp.concatenate([keys_n * m.hmask[head] for head in range(H)], axis=0)
        m.at[row] = dot(stacked, queries).reshape(H, L, L)
        return carry

    lax.fori_loop(0, R // 2, project_row, 0)

    pltpu.make_async_copy(m.b_stage, m.b_recv.at[partner], m.b_sem.at[0]).wait()
    for step in range(1, 8):
        dest = 8 * half + (place + step) % 8
        bias_copy(m.b_recv.at[partner], partner, 7 + step, 2, dest).start()

    lax.fori_loop(R // 2, R, project_row, 0)

    pltpu.make_async_copy(m.b_recv.at[pl.ds(0, 8)], m.b_recv.at[pl.ds(0, 8)], m.b_sem.at[1]).wait()
    pltpu.make_async_copy(m.b_recv.at[pl.ds(0, 7)], m.b_recv.at[pl.ds(0, 7)], m.b_sem.at[2]).wait()
    for head in range(H):
        rows = jnp.concatenate([m.b_recv[peer, R * head : R * (head + 1), :] for peer in range(T)], axis=0)
        m.bias_t[head] = jnp.transpose(rows) * LOG2E

    def attend_row(row, carry):
        values = m.vt[row]
        parts = []
        for head in range(H):
            scores = m.at[row, head] * (INV_ROOT * LOG2E) + m.bias_t[head]
            top = jnp.max(scores, axis=0, keepdims=True)
            weights = jnp.exp2(scores - top)
            weights = weights * (1.0 / total(weights))
            m.at[row, head] = weights
            parts.append(dot(values[HD * head : HD * (head + 1)], weights.astype(BF16)))
        attended = jnp.concatenate(parts, axis=0)
        m.ot[row] = attended
        gated = (m.gt[row] * attended).astype(BF16)
        updated = m.zt[row] + dot(m.wo_t[...], gated) + m.obias_b[...]
        logits = dot(m.wd_t3[...], three(updated))
        m.lgt[row] = logits
        rounded = logits.astype(BF16)
        start = pl.multiple_of(L * row, L)
        m.lgn[pl.ds(start, L), :] = dot_nt(m.eye[...], jnp.concatenate([rounded, rounded], axis=0))
        return carry

    lax.fori_loop(0, R, attend_row, 0)

    low_lanes = lax.broadcasted_iota(I32, (8, L), 1) < NB

    def logits_out(step, carry):
        dest = lax.rem(tile + step, T)
        parts = []
        for index in range(4):
            first = m.lgn[pl.ds(8 * dest + index, 8, stride=L), :]
            second = m.lgn[pl.ds(8 * dest + 4 + index, 8, stride=L), :]
            parts.append(jnp.where(low_lanes, first, second))
        m.c_stage[dest] = jnp.concatenate(parts, axis=0).astype(BF16)

        @pl.when(step > 0)
        def _():
            pltpu.make_async_remote_copy(
                src_ref=m.c_stage.at[dest],
                dst_ref=m.c_recv.at[tile],
                send_sem=m.c_send.at[step],
                recv_sem=m.c_sem,
                device_id=(state, dest),
                device_id_type=MESH,
            ).start()

        @pl.when(step == 0)
        def _():
            pltpu.make_async_copy(m.c_stage.at[tile], m.c_recv.at[tile], m.c_sem).start()

        return carry

    lax.fori_loop(0, T, logits_out, 0)

    pltpu.make_async_copy(m.tg_recv, m.tg_recv, m.tg_sem).wait()
    pltpu.make_async_copy(m.c_recv, m.c_recv, m.c_sem).wait()

    received = [m.c_recv[peer].astype(F32) for peer in range(T)]
    for index in range(4):
        rows = jnp.concatenate([block[8 * index : 8 * (index + 1)] for block in received], axis=0)
        turned = jnp.transpose(rows)
        m.mirror[index] = turned[:NB]
        m.mirror[4 + index] = turned[NB:]

    bins = lax.broadcasted_iota(I32, (NB, L), 0)

    def backward_row(row, carry):
        logits = m.lgt[row] + m.mirror[row] + m.dbias_b[...]
        top = jnp.max(logits, axis=0, keepdims=True)
        expo = jnp.exp(logits - top)
        prob = expo * (1.0 / total(expo))
        wanted = m.tg_recv[row // 2, pl.ds(lax.rem(row, 2), 1), :]
        residual = prob - jnp.where(bins == wanted, 1.0, 0.0)
        pair_grad = dot(m.wd3[...], three(residual))
        m.dp[row] = pair_grad
        out_grad = dot(m.wo_v[...], pair_grad.astype(BF16))
        gate = m.gt[row]
        gated = out_grad * gate
        att_grad = gated.astype(BF16)
        m.d4[row, 3 * C :] = (gated * m.ot[row] * (1.0 - gate)).astype(BF16)
        values_n = m.vn[row]
        queries = m.qt[row]
        keys = m.kt[row]
        stacked = jnp.concatenate([values_n * m.hmask[head] for head in range(H)], axis=0)
        weight_grad = dot(stacked, att_grad)
        for head in range(H):
            span = slice(HD * head, HD * (head + 1))
            weights = m.at[row, head]
            grads = weight_grad[L * head : L * (head + 1)]
            score = weights * (grads - total(weights * grads))
            m.dbt[head] += score
            score_b = score.astype(BF16)
            m.d4[row, HD * head : HD * (head + 1)] = (dot(keys[span], score_b) * INV_ROOT).astype(BF16)
            m.d4[row, C + HD * head : C + HD * (head + 1)] = (
                dot_nt(queries[span], score_b) * INV_ROOT
            ).astype(BF16)
            m.d4[row, 2 * C + HD * head : 2 * C + HD * (head + 1)] = dot_nt(
                att_grad[span], weights.astype(BF16)
            ).astype(BF16)
        return carry

    lax.fori_loop(0, R, backward_row, 0)

    turned = [jnp.transpose(m.dbt[head]) for head in range(H)]
    for peer in range(T):
        m.e_stage[peer] = jnp.concatenate(
            [block[R * peer : R * (peer + 1)] for block in turned], axis=0
        ).astype(BF16)

    def bias_grad_out(step, carry):
        dest = lax.rem(tile + step, T)
        pltpu.make_async_remote_copy(
            src_ref=m.e_stage.at[dest],
            dst_ref=m.e_recv.at[tile],
            send_sem=m.e_send.at[step],
            recv_sem=m.e_sem,
            device_id=(state, dest),
            device_id_type=MESH,
        ).start()
        return carry

    lax.fori_loop(1, T, bias_grad_out, 0)
    pltpu.make_async_copy(m.e_stage.at[tile], m.e_recv.at[tile], m.e_sem).start()

    def back_project(row, carry):
        m.zt[row] = dot(m.w_in[...], m.d4[row])
        return carry

    lax.fori_loop(0, R, back_project, 0)

    pltpu.make_async_copy(m.e_recv, m.e_recv, m.e_sem).wait()
    bias_sum = m.e_recv[0].astype(F32)
    for peer in range(1, T):
        bias_sum = bias_sum + m.e_recv[peer].astype(F32)
    m.dbs[...] = bias_sum

    def finish_pair(pair, carry):
        for side in range(2):
            row = 2 * pair + side
            zn_grad = m.zt[row]
            for head in range(H):
                zn_grad = zn_grad + m.wpb_b[head] * m.dbs[pl.ds(R * head + row, 1), :]
            scaled = zn_grad * m.gain_b[...]
            normed = m.xh[row]
            mean = total(scaled) * (1.0 / C)
            slope = total(scaled * normed) * (1.0 / C)
            result = m.dp[row] + m.inv[row] * (scaled - mean - normed * slope)
            m.grad[row] = dot_nt(m.shift[...], result.astype(BF16))

        def send_state(step, inner):
            dest = lax.rem(state + step, S)
            start = pl.multiple_of(8 * dest, 8)
            upper = m.grad[2 * pair, pl.ds(start, 8), :]
            lower = m.grad[2 * pair + 1, pl.ds(start, 8), :]
            m.f_stage[pair, dest] = jnp.concatenate([upper, lower], axis=0).astype(BF16)
            target = 4 * sub + pair
            here = jnp.logical_and(step == 0, target == tile)

            @pl.when(jnp.logical_not(here))
            def _():
                pltpu.make_async_remote_copy(
                    src_ref=m.f_stage.at[pair, dest],
                    dst_ref=m.f_recv.at[state, band],
                    send_sem=m.f_send.at[pair, step],
                    recv_sem=m.f_sem,
                    device_id=(dest, target),
                    device_id_type=MESH,
                ).start()

            @pl.when(here)
            def _():
                pltpu.make_async_copy(m.f_stage.at[pair, dest], m.f_recv.at[state, band], m.f_sem).start()

            return inner

        lax.fori_loop(0, S, send_state, 0)
        return carry

    lax.fori_loop(0, 4, finish_pair, 0)

    for step in (2, 3, 1):
        tile_copy(step).wait_send()
    for group in range(4):

        @pl.when(4 * group + band != tile)
        def _():
            pltpu.make_async_copy(m.tg_stage.at[0], m.tg_stage.at[0], m.tg_send.at[group]).wait()

    for index in range(15):
        pltpu.make_async_copy(m.b_stage, m.b_stage, m.b_send.at[index]).wait()

    def sent(step, carry):
        pltpu.make_async_copy(m.c_stage.at[0], m.c_stage.at[0], m.c_send.at[step]).wait()
        pltpu.make_async_copy(m.e_stage.at[0], m.e_stage.at[0], m.e_send.at[step]).wait()
        return carry

    lax.fori_loop(1, T, sent, 0)

    pltpu.make_async_copy(m.f_recv, m.f_recv, m.f_sem).wait()
    out[...] = dot(m.spread[...], m.f_recv[...].reshape(S * 64, C)).reshape(out.shape)

    def sent_state(step, carry):
        for pair in range(4):

            @pl.when(jnp.logical_or(step > 0, 4 * sub + pair != tile))
            def _():
                pltpu.make_async_copy(
                    m.f_stage.at[0, 0], m.f_stage.at[0, 0], m.f_send.at[pair, step]
                ).wait()

        return carry

    lax.fori_loop(0, S, sent_state, 0)


def on_device(
    pair_tiles,
    targets,
    offsets,
    ln_gain,
    ln_bias,
    w_query,
    w_key,
    w_value,
    w_pairbias,
    w_gate,
    gate_bias,
    w_output,
    out_bias,
    w_distogram,
    dist_bias,
):
    anywhere = pl.BlockSpec(memory_space=pl.ANY)
    in_specs = [anywhere] * 15
    in_specs[2] = pl.BlockSpec(memory_space=pltpu.SMEM)
    return pl.pallas_call(
        kernel,
        out_shape=jax.ShapeDtypeStruct((8, 1, 2, 2, L // S, C), F32),
        in_specs=in_specs,
        out_specs=pl.BlockSpec(memory_space=pltpu.VMEM),
        scratch_shapes=list(SCRATCH.values()),
        compiler_params=pltpu.CompilerParams(
            collective_id=0, has_side_effects=True, vmem_limit_bytes=40 * 1024 * 1024
        ),
    )(
        pair_tiles,
        targets,
        offsets,
        ln_gain.reshape(1, C),
        ln_bias.reshape(1, C),
        w_query,
        w_key,
        w_value,
        w_pairbias,
        w_gate,
        gate_bias.reshape(1, C),
        w_output,
        out_bias.reshape(1, C),
        w_distogram,
        dist_bias.reshape(1, NB),
    )


def solution(mesh):
    in_specs = (
        P("state", "tile", None, None, None),
        P("state", "tile", None, None, None),
    ) + (P(),) * 13
    out_specs = P(None, "tile", None, None, "state", None)
    return jax.shard_map(
        on_device, mesh=mesh, in_specs=in_specs, out_specs=out_specs, check_vma=False
    )
```

```python
import math

import jax
import jax.numpy as jnp
from jax import lax
from jax.experimental import pallas as pl
from jax.experimental.pallas import tpu as pltpu
from jax.sharding import PartitionSpec as P

C = 128
H = 4
HD = 32
NB = 64
L = 128
S = 16
T = 16
R = 8
F32 = jnp.float32
BF16 = jnp.bfloat16
I32 = jnp.int32
MESH = pl.DeviceIdType.MESH
LOG2E = 1.0 / math.log(2.0)
INV_ROOT = 1.0 / math.sqrt(HD)

SCRATCH = dict(
    gain_v=pltpu.VMEM((1, C), F32),
    lbias_v=pltpu.VMEM((1, C), F32),
    wq_v=pltpu.VMEM((C, C), BF16),
    wk_v=pltpu.VMEM((C, C), BF16),
    wv_v=pltpu.VMEM((C, C), BF16),
    wg_v=pltpu.VMEM((C, C), BF16),
    wo_v=pltpu.VMEM((C, C), BF16),
    wpb_v=pltpu.VMEM((H, C), F32),
    gbias_v=pltpu.VMEM((1, C), F32),
    obias_v=pltpu.VMEM((1, C), F32),
    wd_v=pltpu.VMEM((NB, C), F32),
    dbias_v=pltpu.VMEM((1, NB), F32),
    targets_v=pltpu.VMEM((2, 4, L), I32),
    w_sem=pltpu.SemaphoreType.DMA((13,)),
    eye=pltpu.VMEM((C, C), BF16),
    hmask=pltpu.VMEM((H, C, C), BF16),
    shift=pltpu.VMEM((L, L), BF16),
    spread=pltpu.VMEM((256, S * 64), BF16),
    w_in_t=pltpu.VMEM((4 * C, C), BF16),
    w_in=pltpu.VMEM((C, 4 * C), BF16),
    wo_t=pltpu.VMEM((C, C), BF16),
    wd_t3=pltpu.VMEM((NB, 3 * C), BF16),
    wd3=pltpu.VMEM((C, 3 * NB), BF16),
    gain_b=pltpu.VMEM((C, L), F32),
    lbias_b=pltpu.VMEM((C, L), F32),
    gbias_b=pltpu.VMEM((C, L), F32),
    obias_b=pltpu.VMEM((C, L), F32),
    dbias_b=pltpu.VMEM((NB, L), F32),
    wpb_b=pltpu.VMEM((H, C, L), F32),
    zb=pltpu.VMEM((R, L, C), BF16),
    zt=pltpu.VMEM((R, C, L), F32),
    xh=pltpu.VMEM((R, C, L), F32),
    inv=pltpu.VMEM((R, 1, L), F32),
    znb=pltpu.VMEM((R, C, L), BF16),
    qt=pltpu.VMEM((R, C, L), BF16),
    kt=pltpu.VMEM((R, C, L), BF16),
    vt=pltpu.VMEM((R, C, L), BF16),
    vn=pltpu.VMEM((R, L, C), BF16),
    gt=pltpu.VMEM((R, C, L), F32),
    ot=pltpu.VMEM((R, C, L), F32),
    at=pltpu.VMEM((R, H, L, L), F32),
    bias_t=pltpu.VMEM((H, L, L), F32),
    lgt=pltpu.VMEM((R, NB, L), F32),
    lgn=pltpu.VMEM((R * L, C), F32),
    mirror=pltpu.VMEM((R, NB, L), F32),
    dp=pltpu.VMEM((R, C, L), F32),
    dgt=pltpu.VMEM((R, C, L), BF16),
    dot=pltpu.VMEM((R, C, L), BF16),
    score_b=pltpu.VMEM((R, H, L, L), BF16),
    dbt=pltpu.VMEM((H, L, L), F32),
    dbs=pltpu.VMEM((H * R, L), F32),
    grad=pltpu.VMEM((R, L, C), F32),
    tg_stage=pltpu.VMEM((4, 8, L), I32),
    tg_recv=pltpu.VMEM((4, 8, L), I32),
    b_stage=pltpu.VMEM((H * R, L), F32),
    b_recv=pltpu.VMEM((T, H * R, L), F32),
    c_stage=pltpu.VMEM((T, 32, L), BF16),
    c_recv=pltpu.VMEM((T, 32, L), BF16),
    e_stage=pltpu.VMEM((T, 32, L), BF16),
    e_recv=pltpu.VMEM((T, 32, L), BF16),
    f_stage=pltpu.VMEM((4, S, 16, C), BF16),
    f_recv=pltpu.VMEM((S, 4, 16, C), BF16),
    a_send=pltpu.SemaphoreType.DMA((4,)),
    a_sem=pltpu.SemaphoreType.DMA,
    tg_send=pltpu.SemaphoreType.DMA((4,)),
    tg_sem=pltpu.SemaphoreType.DMA,
    b_send=pltpu.SemaphoreType.DMA((16,)),
    b_sem=pltpu.SemaphoreType.DMA((3,)),
    c_send=pltpu.SemaphoreType.DMA((T,)),
    c_sem=pltpu.SemaphoreType.DMA,
    e_send=pltpu.SemaphoreType.DMA((T,)),
    e_sem=pltpu.SemaphoreType.DMA,
    f_send=pltpu.SemaphoreType.DMA((4, S)),
    f_sem=pltpu.SemaphoreType.DMA,
)
NAMES = tuple(SCRATCH)


class Refs:
    pass


def dot(left, right):
    return jnp.dot(left, right, preferred_element_type=F32)


def dot_nt(left, right):
    return lax.dot_general(left, right, (((1,), (1,)), ((), ())), preferred_element_type=F32)


def halves(values):
    high = values.astype(BF16)
    low = (values - high.astype(F32)).astype(BF16)
    return high, low


def three(values):
    high, low = halves(values)
    return jnp.concatenate([high, low, high], axis=0)


def total(values):
    return jnp.sum(values, axis=0, keepdims=True)


def column(row):
    width = row.shape[1]
    return jnp.transpose(jnp.broadcast_to(row, (L, width)))


def kernel(
    tiles,
    targets,
    offsets,
    gain,
    lbias,
    wq,
    wk,
    wv,
    wpb,
    wg,
    gbias,
    wo,
    obias,
    wd,
    dbias,
    out,
    *scratch,
):
    m = Refs()
    for name, ref in zip(NAMES, scratch):
        setattr(m, name, ref)
    state = lax.axis_index("state")
    tile = lax.axis_index("tile")
    band = tile // 4
    sub = tile % 4

    barrier = pltpu.get_barrier_semaphore()

    def greet_tile(step, carry):
        peer = lax.rem(tile + step, T)
        pl.semaphore_signal(barrier, inc=1, device_id=(state, peer), device_id_type=MESH)
        return carry

    lax.fori_loop(1, T, greet_tile, 0)

    def greet_state(step, carry):
        peer = lax.rem(state + step, S)
        for group in range(4):
            pl.semaphore_signal(
                barrier, inc=1, device_id=(peer, 4 * group + band), device_id_type=MESH
            )
        return carry

    lax.fori_loop(1, S, greet_state, 0)

    loads = []
    for index, (source, target) in enumerate(
        [
            (gain, m.gain_v),
            (lbias, m.lbias_v),
            (wq, m.wq_v),
            (wk, m.wk_v),
            (wv, m.wv_v),
            (wg, m.wg_v),
            (wo, m.wo_v),
            (wpb, m.wpb_v),
            (gbias, m.gbias_v),
            (obias, m.obias_v),
            (wd, m.wd_v),
            (dbias, m.dbias_v),
            (targets.at[0, 0], m.targets_v),
        ]
    ):
        load = pltpu.make_async_copy(source, target, m.w_sem.at[index])
        load.start()
        loads.append(load)

    pl.semaphore_wait(barrier, T - 1 + 4 * (S - 1))

    def tile_copy(step):
        other = lax.rem(sub + step, 4)
        return pltpu.make_async_remote_copy(
            src_ref=tiles.at[0, 0, pl.ds(R * other, R)],
            dst_ref=m.zb.at[:, pl.ds(pl.multiple_of(32 * sub, 32), 32), :],
            send_sem=m.a_send.at[step],
            recv_sem=m.a_sem,
            device_id=(state, 4 * band + other),
            device_id_type=MESH,
        )

    for step in (2, 3, 1):
        tile_copy(step).start()
    pltpu.make_async_copy(
        tiles.at[0, 0, pl.ds(R * sub, R)],
        m.zb.at[:, pl.ds(pl.multiple_of(32 * sub, 32), 32), :],
        m.a_sem,
    ).start()
    rows_i = lax.broadcasted_iota(I32, (C, C), 0)
    cols_i = lax.broadcasted_iota(I32, (C, C), 1)
    m.eye[...] = jnp.where(rows_i == cols_i, 1.0, 0.0).astype(BF16)
    for head in range(H):
        m.hmask[head] = jnp.where(cols_i // HD == head, 1.0, 0.0).astype(BF16)
    m.shift[...] = jnp.where(((rows_i - offsets[state] + L) & (L - 1)) == cols_i, 1.0, 0.0).astype(BF16)
    rows_o = lax.broadcasted_iota(I32, (256, L), 0)
    cols_o = lax.broadcasted_iota(I32, (256, L), 1)
    row_in = 8 * ((rows_o >> 4) & 1) + (rows_o & 7)
    same_row = row_in == (cols_o & 15)
    band_gap = 32 * ((rows_o >> 5) - ((cols_o >> 4) & 3))
    upper_half = (rows_o >> 3) & 1
    for index in range(S // 2):
        offset = jnp.where(cols_o < 64, offsets[2 * index], offsets[2 * index + 1])
        wrapped = jnp.where(offset > 8 * state, 1, 0)
        chosen = same_row & (band_gap == offset) & (upper_half == wrapped)
        m.spread[:, L * index : L * (index + 1)] = jnp.where(chosen, 1.0, 0.0).astype(BF16)
    for load in loads:
        load.wait()
    for group in range(4):
        m.tg_stage[group] = jnp.concatenate([m.targets_v[:, group, :]] * 4, axis=0)
    for group in range(4):
        dest = 4 * group + band

        @pl.when(dest != tile)
        def _():
            pltpu.make_async_remote_copy(
                src_ref=m.tg_stage.at[group],
                dst_ref=m.tg_recv.at[sub],
                send_sem=m.tg_send.at[group],
                recv_sem=m.tg_sem,
                device_id=(state, dest),
                device_id_type=MESH,
            ).start()

        @pl.when(dest == tile)
        def _():
            pltpu.make_async_copy(m.tg_stage.at[group], m.tg_recv.at[sub], m.tg_sem).start()

    eye = m.eye[...]
    for index, ref in enumerate((m.wq_v, m.wk_v, m.wv_v, m.wg_v)):
        weight = ref[...]
        m.w_in[:, C * index : C * (index + 1)] = weight
        m.w_in_t[C * index : C * (index + 1), :] = dot_nt(eye, weight).astype(BF16)
    m.wo_t[...] = dot_nt(eye, m.wo_v[...]).astype(BF16)
    head_w = m.wd_v[...]
    high, low = halves(2.0 * jnp.transpose(head_w))
    m.wd3[...] = jnp.concatenate([high, high, low], axis=1)
    high, low = halves(head_w - total(head_w) * (1.0 / NB))
    m.wd_t3[...] = jnp.concatenate([high, high, low], axis=1)
    m.gain_b[...] = column(m.gain_v[...])
    m.lbias_b[...] = column(m.lbias_v[...])
    m.gbias_b[...] = column(m.gbias_v[...])
    m.obias_b[...] = column(m.obias_v[...])
    m.dbias_b[...] = column(m.dbias_v[...])
    for head in range(H):
        m.wpb_b[head] = column(m.wpb_v[head : head + 1])
    m.dbt[...] = jnp.zeros_like(m.dbt)

    pltpu.make_async_copy(m.zb, m.zb, m.a_sem).wait()

    def norm_row(row, carry):
        z = dot_nt(m.eye[...], m.zb[row])
        centre = z - total(z) * (1.0 / C)
        inverse = lax.rsqrt(total(centre * centre) * (1.0 / C) + 1e-05)
        normed = centre * inverse
        zn = normed * m.gain_b[...] + m.lbias_b[...]
        m.zt[row] = z
        m.xh[row] = normed
        m.inv[row] = inverse
        m.znb[row] = zn.astype(BF16)
        for head in range(H):
            m.b_stage[pl.ds(R * head + row, 1), :] = total(zn * m.wpb_b[head])
        return carry

    lax.fori_loop(0, R, norm_row, 0, unroll=True)

    half = tile // 8
    place = tile % 8
    partner = 8 * (1 - half) + place

    def bias_copy(source, slot, index, sem, dest):
        return pltpu.make_async_remote_copy(
            src_ref=source,
            dst_ref=m.b_recv.at[slot],
            send_sem=m.b_send.at[index],
            recv_sem=m.b_sem.at[sem],
            device_id=(state, dest),
            device_id_type=MESH,
        )

    bias_copy(m.b_stage, tile, 0, 0, partner).start()
    for step in range(1, 8):
        dest = 8 * half + (place + step) % 8
        bias_copy(m.b_stage, tile, step, 1, dest).start()
    pltpu.make_async_copy(m.b_stage, m.b_recv.at[tile], m.b_sem.at[1]).start()

    def project_row(row, carry):
        proj = dot(m.w_in_t[...], m.znb[row])
        keys = proj[C : 2 * C].astype(BF16)
        values = proj[2 * C : 3 * C].astype(BF16)
        queries = proj[:C].astype(BF16)
        m.qt[row] = queries
        m.kt[row] = keys
        m.vt[row] = values
        m.gt[row] = jax.nn.sigmoid(proj[3 * C :] + m.gbias_b[...])
        keys_n = dot_nt(m.eye[...], keys).astype(BF16)
        m.vn[row] = dot_nt(m.eye[...], values).astype(BF16)
        stacked = jnp.concatenate([keys_n * m.hmask[head] for head in range(H)], axis=0)
        m.at[row] = dot(stacked, queries).reshape(H, L, L)
        return carry

    lax.fori_loop(0, R // 2, project_row, 0, unroll=True)

    pltpu.make_async_copy(m.b_stage, m.b_recv.at[partner], m.b_sem.at[0]).wait()
    for step in range(1, 8):
        dest = 8 * half + (place + step) % 8
        bias_copy(m.b_recv.at[partner], partner, 7 + step, 2, dest).start()

    lax.fori_loop(R // 2, R, project_row, 0, unroll=True)

    pltpu.make_async_copy(m.b_recv.at[pl.ds(0, 8)], m.b_recv.at[pl.ds(0, 8)], m.b_sem.at[1]).wait()
    pltpu.make_async_copy(m.b_recv.at[pl.ds(0, 7)], m.b_recv.at[pl.ds(0, 7)], m.b_sem.at[2]).wait()
    for head in range(H):
        rows = jnp.concatenate([m.b_recv[peer, R * head : R * (head + 1), :] for peer in range(T)], axis=0)
        m.bias_t[head] = jnp.transpose(rows) * LOG2E

    def attend_row(row, carry):
        values = m.vt[row]
        parts = []
        for head in range(H):
            scores = m.at[row, head] * (INV_ROOT * LOG2E) + m.bias_t[head]
            top = jnp.max(scores, axis=0, keepdims=True)
            weights = jnp.exp2(scores - top)
            weights = weights * (1.0 / total(weights))
            m.at[row, head] = weights
            parts.append(dot(values[HD * head : HD * (head + 1)], weights.astype(BF16)))
        attended = jnp.concatenate(parts, axis=0)
        m.ot[row] = attended
        gated = (m.gt[row] * attended).astype(BF16)
        updated = m.zt[row] + dot(m.wo_t[...], gated) + m.obias_b[...]
        logits = dot(m.wd_t3[...], three(updated))
        m.lgt[row] = logits
        rounded = logits.astype(BF16)
        start = pl.multiple_of(L * row, L)
        m.lgn[pl.ds(start, L), :] = dot_nt(m.eye[...], jnp.concatenate([rounded, rounded], axis=0))
        return carry

    lax.fori_loop(0, R, attend_row, 0, unroll=True)

    order = [(1, d) for d in (4, 3, 5, 2, 6, 1, 7, 0)] + [(0, d) for d in (4, 3, 5, 2, 6, 1, 7, 0)]

    def peer_of(flip, step):
        return 8 * (half + flip * (1 - 2 * half)) + (place + step) % 8

    low_lanes = lax.broadcasted_iota(I32, (8, L), 1) < NB

    for index, (flip, step) in enumerate(order):
        dest = peer_of(flip, step)
        parts = []
        for column_in in range(4):
            first = m.lgn[pl.ds(8 * dest + column_in, 8, stride=L), :]
            second = m.lgn[pl.ds(8 * dest + 4 + column_in, 8, stride=L), :]
            parts.append(jnp.where(low_lanes, first, second))
        m.c_stage[dest] = jnp.concatenate(parts, axis=0).astype(BF16)
        if index < T - 1:
            pltpu.make_async_remote_copy(
                src_ref=m.c_stage.at[dest],
                dst_ref=m.c_recv.at[tile],
                send_sem=m.c_send.at[index],
                recv_sem=m.c_sem,
                device_id=(state, dest),
                device_id_type=MESH,
            ).start()
        else:
            pltpu.make_async_copy(m.c_stage.at[tile], m.c_recv.at[tile], m.c_sem).start()

    pltpu.make_async_copy(m.tg_recv, m.tg_recv, m.tg_sem).wait()
    pltpu.make_async_copy(m.c_recv, m.c_recv, m.c_sem).wait()

    received = [m.c_recv[peer].astype(F32) for peer in range(T)]
    for index in range(4):
        rows = jnp.concatenate([block[8 * index : 8 * (index + 1)] for block in received], axis=0)
        turned = jnp.transpose(rows)
        m.mirror[index] = turned[:NB]
        m.mirror[4 + index] = turned[NB:]

    bins = lax.broadcasted_iota(I32, (NB, L), 0)

    def backward_row(row, carry):
        logits = m.lgt[row] + m.mirror[row] + m.dbias_b[...]
        top = jnp.max(logits, axis=0, keepdims=True)
        expo = jnp.exp(logits - top)
        prob = expo * (1.0 / total(expo))
        wanted = m.tg_recv[row // 2, pl.ds(lax.rem(row, 2), 1), :]
        residual = prob - jnp.where(bins == wanted, 1.0, 0.0)
        pair_grad = dot(m.wd3[...], three(residual))
        m.dp[row] = pair_grad
        out_grad = dot(m.wo_v[...], pair_grad.astype(BF16))
        gate = m.gt[row]
        gated = out_grad * gate
        att_grad = gated.astype(BF16)
        m.dot[row] = att_grad
        m.dgt[row] = (gated * m.ot[row] * (1.0 - gate)).astype(BF16)
        values_n = m.vn[row]
        stacked = jnp.concatenate([values_n * m.hmask[head] for head in range(H)], axis=0)
        weight_grad = dot(stacked, att_grad)
        for head in range(H):
            span = slice(HD * head, HD * (head + 1))
            weights = m.at[row, head]
            grads = weight_grad[L * head : L * (head + 1)]
            score = weights * (grads - total(weights * grads))
            m.dbt[head] += score
            m.score_b[row, head] = score.astype(BF16)
        return carry

    lax.fori_loop(0, R, backward_row, 0, unroll=True)

    turned = [jnp.transpose(m.dbt[head]) for head in range(H)]
    for peer in range(T):
        m.e_stage[peer] = jnp.concatenate(
            [block[R * peer : R * (peer + 1)] for block in turned], axis=0
        ).astype(BF16)

    for index, (flip, step) in enumerate(order[:-1]):
        dest = peer_of(flip, step)
        pltpu.make_async_remote_copy(
            src_ref=m.e_stage.at[dest],
            dst_ref=m.e_recv.at[tile],
            send_sem=m.e_send.at[index],
            recv_sem=m.e_sem,
            device_id=(state, dest),
            device_id_type=MESH,
        ).start()
    pltpu.make_async_copy(m.e_stage.at[tile], m.e_recv.at[tile], m.e_sem).start()

    def back_project(row, carry):
        queries = m.qt[row]
        keys = m.kt[row]
        att_grad = m.dot[row]
        spans = [slice(HD * head, HD * (head + 1)) for head in range(H)]
        scores = [m.score_b[row, head] for head in range(H)]
        parts = [dot(keys[span], score) * INV_ROOT for span, score in zip(spans, scores)]
        parts += [dot_nt(queries[span], score) * INV_ROOT for span, score in zip(spans, scores)]
        parts += [dot_nt(att_grad[span], m.at[row, head].astype(BF16)) for head, span in enumerate(spans)]
        grads = jnp.concatenate(parts, axis=0).astype(BF16)
        m.zt[row] = dot(m.w_in[...], jnp.concatenate([grads, m.dgt[row]], axis=0))
        return carry

    lax.fori_loop(0, R, back_project, 0, unroll=True)

    pltpu.make_async_copy(m.e_recv, m.e_recv, m.e_sem).wait()
    bias_sum = m.e_recv[0].astype(F32)
    for peer in range(1, T):
        bias_sum = bias_sum + m.e_recv[peer].astype(F32)
    m.dbs[...] = bias_sum

    def finish_pair(pair, carry):
        for side in range(2):
            row = 2 * pair + side
            zn_grad = m.zt[row]
            for head in range(H):
                zn_grad = zn_grad + m.wpb_b[head] * m.dbs[pl.ds(R * head + row, 1), :]
            scaled = zn_grad * m.gain_b[...]
            normed = m.xh[row]
            mean = total(scaled) * (1.0 / C)
            slope = total(scaled * normed) * (1.0 / C)
            result = m.dp[row] + m.inv[row] * (scaled - mean - normed * slope)
            m.grad[row] = dot_nt(m.shift[...], result.astype(BF16))

        def send_state(step, inner):
            dest = lax.rem(state + step, S)
            start = pl.multiple_of(8 * dest, 8)
            upper = m.grad[2 * pair, pl.ds(start, 8), :]
            lower = m.grad[2 * pair + 1, pl.ds(start, 8), :]
            m.f_stage[pair, dest] = jnp.concatenate([upper, lower], axis=0).astype(BF16)
            target = 4 * sub + pair
            here = jnp.logical_and(step == 0, target == tile)

            @pl.when(jnp.logical_not(here))
            def _():
                pltpu.make_async_remote_copy(
                    src_ref=m.f_stage.at[pair, dest],
                    dst_ref=m.f_recv.at[state, band],
                    send_sem=m.f_send.at[pair, step],
                    recv_sem=m.f_sem,
                    device_id=(dest, target),
                    device_id_type=MESH,
                ).start()

            @pl.when(here)
            def _():
                pltpu.make_async_copy(m.f_stage.at[pair, dest], m.f_recv.at[state, band], m.f_sem).start()

            return inner

        lax.fori_loop(0, S, send_state, 0)
        return carry

    lax.fori_loop(0, 4, finish_pair, 0, unroll=True)

    for step in (2, 3, 1):
        tile_copy(step).wait_send()
    for group in range(4):

        @pl.when(4 * group + band != tile)
        def _():
            pltpu.make_async_copy(m.tg_stage.at[0], m.tg_stage.at[0], m.tg_send.at[group]).wait()

    for index in range(15):
        pltpu.make_async_copy(m.b_stage, m.b_stage, m.b_send.at[index]).wait()

    def sent(step, carry):
        pltpu.make_async_copy(m.c_stage.at[0], m.c_stage.at[0], m.c_send.at[step]).wait()
        pltpu.make_async_copy(m.e_stage.at[0], m.e_stage.at[0], m.e_send.at[step]).wait()
        return carry

    lax.fori_loop(0, T - 1, sent, 0)

    pltpu.make_async_copy(m.f_recv, m.f_recv, m.f_sem).wait()
    out[...] = dot(m.spread[...], m.f_recv[...].reshape(S * 64, C)).reshape(out.shape)

    def sent_state(step, carry):
        for pair in range(4):

            @pl.when(jnp.logical_or(step > 0, 4 * sub + pair != tile))
            def _():
                pltpu.make_async_copy(
                    m.f_stage.at[0, 0], m.f_stage.at[0, 0], m.f_send.at[pair, step]
                ).wait()

        return carry

    lax.fori_loop(0, S, sent_state, 0)


def on_device(
    pair_tiles,
    targets,
    offsets,
    ln_gain,
    ln_bias,
    w_query,
    w_key,
    w_value,
    w_pairbias,
    w_gate,
    gate_bias,
    w_output,
    out_bias,
    w_distogram,
    dist_bias,
):
    anywhere = pl.BlockSpec(memory_space=pltpu.HBM)
    in_specs = [anywhere] * 15
    in_specs[2] = pl.BlockSpec(memory_space=pltpu.SMEM)
    return pl.pallas_call(
        kernel,
        out_shape=jax.ShapeDtypeStruct((8, 1, 2, 2, L // S, C), F32),
        in_specs=in_specs,
        out_specs=pl.BlockSpec(memory_space=pltpu.VMEM),
        scratch_shapes=list(SCRATCH.values()),
        compiler_params=pltpu.CompilerParams(
            collective_id=0, has_side_effects=True, vmem_limit_bytes=64 * 1024 * 1024
        ),
    )(
        pair_tiles,
        targets,
        offsets,
        ln_gain.reshape(1, C),
        ln_bias.reshape(1, C),
        w_query,
        w_key,
        w_value,
        w_pairbias.T,
        w_gate,
        gate_bias.reshape(1, C),
        w_output,
        out_bias.reshape(1, C),
        w_distogram.T,
        dist_bias.reshape(1, NB),
    )


def solution(mesh):
    in_specs = (
        P("state", "tile", None, None, None),
        P("state", "tile", None, None, None),
    ) + (P(),) * 13
    out_specs = P(None, "tile", None, None, "state", None)
    return jax.shard_map(
        on_device, mesh=mesh, in_specs=in_specs, out_specs=out_specs, check_vma=False
    )
```

```python
import math

import jax
import jax.numpy as jnp
from jax import lax
from jax.experimental import pallas as pl
from jax.experimental.pallas import tpu as pltpu
from jax.sharding import PartitionSpec as P

C = 128
H = 4
HD = 32
NB = 64
L = 128
S = 16
T = 16
R = 8
F32 = jnp.float32
BF16 = jnp.bfloat16
I32 = jnp.int32
MESH = pl.DeviceIdType.MESH
LOG2E = 1.0 / math.log(2.0)
INV_ROOT = 1.0 / math.sqrt(HD)

SCRATCH = dict(
    gain_v=pltpu.VMEM((1, C), F32),
    lbias_v=pltpu.VMEM((1, C), F32),
    wq_v=pltpu.VMEM((C, C), BF16),
    wk_v=pltpu.VMEM((C, C), BF16),
    wv_v=pltpu.VMEM((C, C), BF16),
    wg_v=pltpu.VMEM((C, C), BF16),
    wo_v=pltpu.VMEM((C, C), BF16),
    wpb_v=pltpu.VMEM((H, C), F32),
    gbias_v=pltpu.VMEM((1, C), F32),
    obias_v=pltpu.VMEM((1, C), F32),
    wd_v=pltpu.VMEM((NB, C), F32),
    dbias_v=pltpu.VMEM((1, NB), F32),
    targets_v=pltpu.VMEM((2, 4, L), I32),
    w_sem=pltpu.SemaphoreType.DMA((14,)),
    eye=pltpu.VMEM((C, C), BF16),
    hmask=pltpu.VMEM((H, C, C), BF16),
    shift=pltpu.VMEM((L, L), BF16),
    spread=pltpu.VMEM((256, S * 64), BF16),
    w_in_t=pltpu.VMEM((4 * C, C), BF16),
    w_in=pltpu.VMEM((C, 4 * C), BF16),
    wo_t=pltpu.VMEM((C, C), BF16),
    wd_t3=pltpu.VMEM((NB, 3 * C), BF16),
    wd3=pltpu.VMEM((C, 3 * NB), BF16),
    gain_b=pltpu.VMEM((C, L), F32),
    lbias_b=pltpu.VMEM((C, L), F32),
    gbias_b=pltpu.VMEM((C, L), F32),
    obias_b=pltpu.VMEM((C, L), F32),
    dbias_b=pltpu.VMEM((NB, L), F32),
    wpb_b=pltpu.VMEM((H, C, L), F32),
    zb=pltpu.VMEM((R, L, C), BF16),
    zt=pltpu.VMEM((R, C, L), F32),
    xh=pltpu.VMEM((R, C, L), F32),
    inv=pltpu.VMEM((R, 1, L), F32),
    znb=pltpu.VMEM((R, C, L), BF16),
    qt=pltpu.VMEM((R, C, L), BF16),
    kt=pltpu.VMEM((R, C, L), BF16),
    vt=pltpu.VMEM((R, C, L), BF16),
    vn=pltpu.VMEM((R, L, C), BF16),
    gt=pltpu.VMEM((R, C, L), F32),
    ot=pltpu.VMEM((R, C, L), F32),
    at=pltpu.VMEM((R, H, L, L), F32),
    bias_t=pltpu.VMEM((H, L, L), F32),
    lgt=pltpu.VMEM((R, NB, L), F32),
    lgn=pltpu.VMEM((R * L, C), F32),
    mirror=pltpu.VMEM((R, NB, L), F32),
    dp=pltpu.VMEM((R, C, L), F32),
    dgt=pltpu.VMEM((R, C, L), BF16),
    dot=pltpu.VMEM((R, C, L), BF16),
    score_b=pltpu.VMEM((R, H, L, L), BF16),
    dbt=pltpu.VMEM((H, L, L), F32),
    dbs=pltpu.VMEM((H * R, L), F32),
    grad=pltpu.VMEM((R, L, C), F32),
    tg_stage=pltpu.VMEM((4, 8, L), I32),
    tg_recv=pltpu.VMEM((4, 8, L), I32),
    tile_v=pltpu.VMEM((32, 32, C), BF16),
    b_rows=pltpu.VMEM((H * R, L), F32),
    b_stage=pltpu.VMEM((32, L), F32),
    b_recv=pltpu.VMEM((T, 32, L), F32),
    c_stage=pltpu.VMEM((T, 32, L), BF16),
    c_recv=pltpu.VMEM((T, 32, L), BF16),
    e_stage=pltpu.VMEM((T, 32, L), BF16),
    e_recv=pltpu.VMEM((T, 32, L), BF16),
    f_stage=pltpu.VMEM((4, S, 16, C), BF16),
    f_recv=pltpu.VMEM((S, 4, 16, C), BF16),
    a_send=pltpu.SemaphoreType.DMA((4,)),
    a_sem=pltpu.SemaphoreType.DMA,
    tg_send=pltpu.SemaphoreType.DMA((4,)),
    tg_sem=pltpu.SemaphoreType.DMA,
    b_send=pltpu.SemaphoreType.DMA((16,)),
    b_sem=pltpu.SemaphoreType.DMA((3,)),
    c_send=pltpu.SemaphoreType.DMA((T,)),
    c_sem=pltpu.SemaphoreType.DMA,
    e_send=pltpu.SemaphoreType.DMA((T,)),
    e_sem=pltpu.SemaphoreType.DMA,
    f_send=pltpu.SemaphoreType.DMA((4, S)),
    f_sem=pltpu.SemaphoreType.DMA,
)
NAMES = tuple(SCRATCH)


class Refs:
    pass


def dot(left, right):
    return jnp.dot(left, right, preferred_element_type=F32)


def dot_nt(left, right):
    return lax.dot_general(left, right, (((1,), (1,)), ((), ())), preferred_element_type=F32)


def halves(values):
    high = values.astype(BF16)
    low = (values - high.astype(F32)).astype(BF16)
    return high, low


def three(values):
    high, low = halves(values)
    return jnp.concatenate([high, low, high], axis=0)


def total(values):
    return jnp.sum(values, axis=0, keepdims=True)


def swap(index):
    return 2 * (index % 2) + index // 2


def block_of(device):
    return device - device % 4 + swap(device % 4)


def column(row):
    width = row.shape[1]
    return jnp.transpose(jnp.broadcast_to(row, (L, width)))


def kernel(
    tiles,
    targets,
    offsets,
    gain,
    lbias,
    wq,
    wk,
    wv,
    wpb,
    wg,
    gbias,
    wo,
    obias,
    wd,
    dbias,
    out,
    *scratch,
):
    m = Refs()
    for name, ref in zip(NAMES, scratch):
        setattr(m, name, ref)
    state = lax.axis_index("state")
    tile = lax.axis_index("tile")
    band = tile // 4
    sub = tile % 4
    group = swap(sub)
    block = 4 * band + group

    barrier = pltpu.get_barrier_semaphore()

    def greet_tile(step, carry):
        peer = lax.rem(tile + step, T)
        pl.semaphore_signal(barrier, inc=1, device_id=(state, peer), device_id_type=MESH)
        return carry

    lax.fori_loop(1, T, greet_tile, 0)

    def greet_state(step, carry):
        peer = lax.rem(state + step, S)
        for index in range(4):
            pl.semaphore_signal(
                barrier, inc=1, device_id=(peer, 4 * index + swap(band)), device_id_type=MESH
            )
        return carry

    lax.fori_loop(1, S, greet_state, 0)

    loads = []
    for index, (source, target) in enumerate(
        [
            (gain, m.gain_v),
            (lbias, m.lbias_v),
            (wq, m.wq_v),
            (wk, m.wk_v),
            (wv, m.wv_v),
            (wg, m.wg_v),
            (wo, m.wo_v),
            (wpb, m.wpb_v),
            (gbias, m.gbias_v),
            (obias, m.obias_v),
            (wd, m.wd_v),
            (dbias, m.dbias_v),
            (targets.at[0, 0], m.targets_v),
            (tiles.at[0, 0], m.tile_v),
        ]
    ):
        load = pltpu.make_async_copy(source, target, m.w_sem.at[index])
        load.start()
        loads.append(load)

    rows_i = lax.broadcasted_iota(I32, (C, C), 0)
    cols_i = lax.broadcasted_iota(I32, (C, C), 1)
    m.eye[...] = jnp.where(rows_i == cols_i, 1.0, 0.0).astype(BF16)
    for head in range(H):
        m.hmask[head] = jnp.where(cols_i // HD == head, 1.0, 0.0).astype(BF16)
    early = (0, 1, 7, 13)
    late_loads = [load for index, load in enumerate(loads) if index not in early]
    for index in early:
        loads[index].wait()
    eye = m.eye[...]
    m.gain_b[...] = column(m.gain_v[...])
    m.lbias_b[...] = column(m.lbias_v[...])
    for head in range(H):
        m.wpb_b[head] = column(m.wpb_v[head : head + 1])

    for index in range(R):
        z = dot_nt(eye, m.tile_v[4 * index : 4 * (index + 1)].reshape(L, C))
        centre = z - total(z) * (1.0 / C)
        inverse = lax.rsqrt(total(centre * centre) * (1.0 / C) + 1e-05)
        zn = centre * inverse * m.gain_b[...] + m.lbias_b[...]
        for head in range(H):
            m.b_rows[R * head + index : R * head + index + 1, :] = total(zn * m.wpb_b[head]) * LOG2E
    turned = jnp.transpose(m.b_rows[...])
    rows_s = lax.broadcasted_iota(I32, (32, L), 0)
    cols_s = lax.broadcasted_iota(I32, (32, L), 1)
    tile_bias = jnp.zeros((32, L), F32)
    for part in range(3):
        piece = turned.astype(BF16)
        turned = turned - piece.astype(F32)
        for index in range(4):
            lane = 32 * (rows_s // R) + 4 * (rows_s % R) + index
            place_it = jnp.where(lane == cols_s, 1.0, 0.0).astype(BF16)
            tile_bias = tile_bias + dot(piece[32 * index : 32 * (index + 1)], place_it)
    m.b_stage[...] = tile_bias

    pl.semaphore_wait(barrier, T - 1 + 4 * (S - 1))

    def tile_copy(step):
        other = lax.rem(sub + step, 4)
        return pltpu.make_async_remote_copy(
            src_ref=tiles.at[0, 0, pl.ds(R * swap(other), R)],
            dst_ref=m.zb.at[:, pl.ds(pl.multiple_of(32 * sub, 32), 32), :],
            send_sem=m.a_send.at[step],
            recv_sem=m.a_sem,
            device_id=(state, 4 * band + other),
            device_id_type=MESH,
        )

    half = tile // 8
    place = tile % 8
    partner = 8 * (1 - half) + place

    def bias_copy(source, slot, index, sem, dest):
        return pltpu.make_async_remote_copy(
            src_ref=source,
            dst_ref=m.b_recv.at[slot],
            send_sem=m.b_send.at[index],
            recv_sem=m.b_sem.at[sem],
            device_id=(state, dest),
            device_id_type=MESH,
        )

    bias_copy(m.b_stage, tile, 0, 0, partner).start()
    for step in (2, 3, 1):
        tile_copy(step).start()
    pltpu.make_async_copy(
        tiles.at[0, 0, pl.ds(R * group, R)],
        m.zb.at[:, pl.ds(pl.multiple_of(32 * sub, 32), 32), :],
        m.a_sem,
    ).start()
    for step in range(1, 8):
        dest = 8 * half + (place + step) % 8
        bias_copy(m.b_stage, tile, step, 1, dest).start()
    pltpu.make_async_copy(m.b_stage, m.b_recv.at[tile], m.b_sem.at[1]).start()

    m.shift[...] = jnp.where(((rows_i - offsets[state] + L) & (L - 1)) == cols_i, 1.0, 0.0).astype(BF16)
    rows_o = lax.broadcasted_iota(I32, (256, L), 0)
    cols_o = lax.broadcasted_iota(I32, (256, L), 1)
    row_in = 8 * ((rows_o >> 4) & 1) + (rows_o & 7)
    same_row = row_in == (cols_o & 15)
    band_gap = 32 * ((rows_o >> 5) - ((cols_o >> 4) & 3))
    upper_half = (rows_o >> 3) & 1
    for index in range(S // 2):
        offset = jnp.where(cols_o < 64, offsets[2 * index], offsets[2 * index + 1])
        wrapped = jnp.where(offset > 8 * state, 1, 0)
        chosen = same_row & (band_gap == offset) & (upper_half == wrapped)
        m.spread[:, L * index : L * (index + 1)] = jnp.where(chosen, 1.0, 0.0).astype(BF16)
    for load in late_loads:
        load.wait()
    for index in range(4):
        m.tg_stage[index] = jnp.concatenate([m.targets_v[:, index, :]] * 4, axis=0)
    for index in range(4):
        dest = 4 * index + swap(band)

        @pl.when(dest != tile)
        def _():
            pltpu.make_async_remote_copy(
                src_ref=m.tg_stage.at[index],
                dst_ref=m.tg_recv.at[sub],
                send_sem=m.tg_send.at[index],
                recv_sem=m.tg_sem,
                device_id=(state, dest),
                device_id_type=MESH,
            ).start()

        @pl.when(dest == tile)
        def _():
            pltpu.make_async_copy(m.tg_stage.at[index], m.tg_recv.at[sub], m.tg_sem).start()

    for index, ref in enumerate((m.wq_v, m.wk_v, m.wv_v, m.wg_v)):
        weight = ref[...]
        m.w_in[:, C * index : C * (index + 1)] = weight
        m.w_in_t[C * index : C * (index + 1), :] = dot_nt(eye, weight).astype(BF16)
    m.wo_t[...] = dot_nt(eye, m.wo_v[...]).astype(BF16)
    head_w = m.wd_v[...]
    high, low = halves(2.0 * jnp.transpose(head_w))
    m.wd3[...] = jnp.concatenate([high, high, low], axis=1)
    high, low = halves(head_w - total(head_w) * (1.0 / NB))
    m.wd_t3[...] = jnp.concatenate([high, high, low], axis=1)
    m.gbias_b[...] = column(m.gbias_v[...])
    m.obias_b[...] = column(m.obias_v[...])
    m.dbias_b[...] = column(m.dbias_v[...])
    m.dbt[...] = jnp.zeros_like(m.dbt)

    pltpu.make_async_copy(m.zb, m.zb, m.a_sem).wait()

    def norm_row(row, carry):
        z = dot_nt(m.eye[...], m.zb[row])
        centre = z - total(z) * (1.0 / C)
        inverse = lax.rsqrt(total(centre * centre) * (1.0 / C) + 1e-05)
        normed = centre * inverse
        zn = normed * m.gain_b[...] + m.lbias_b[...]
        m.zt[row] = z
        m.xh[row] = normed
        m.inv[row] = inverse
        m.znb[row] = zn.astype(BF16)
        return carry

    lax.fori_loop(0, R, norm_row, 0, unroll=True)

    def project_row(row, carry):
        proj = dot(m.w_in_t[...], m.znb[row])
        keys = proj[C : 2 * C].astype(BF16)
        values = proj[2 * C : 3 * C].astype(BF16)
        queries = proj[:C].astype(BF16)
        m.qt[row] = queries
        m.kt[row] = keys
        m.vt[row] = values
        m.gt[row] = jax.nn.sigmoid(proj[3 * C :] + m.gbias_b[...])
        keys_n = dot_nt(m.eye[...], keys).astype(BF16)
        m.vn[row] = dot_nt(m.eye[...], values).astype(BF16)
        stacked = jnp.concatenate([keys_n * m.hmask[head] for head in range(H)], axis=0)
        m.at[row] = dot(stacked, queries).reshape(H, L, L)
        return carry

    pltpu.make_async_copy(m.b_stage, m.b_recv.at[partner], m.b_sem.at[0]).wait()
    for step in range(1, 8):
        dest = 8 * half + (place + step) % 8
        bias_copy(m.b_recv.at[partner], partner, 7 + step, 2, dest).start()

    lax.fori_loop(0, R, project_row, 0, unroll=True)

    pltpu.make_async_copy(m.b_recv.at[pl.ds(0, 8)], m.b_recv.at[pl.ds(0, 8)], m.b_sem.at[1]).wait()
    pltpu.make_async_copy(m.b_recv.at[pl.ds(0, 7)], m.b_recv.at[pl.ds(0, 7)], m.b_sem.at[2]).wait()
    bands = [m.b_recv[4 * index : 4 * (index + 1)].reshape(L, L) for index in range(4)]
    for head in range(H):
        m.bias_t[head] = jnp.concatenate([part[:, 32 * head : 32 * (head + 1)] for part in bands], axis=1)

    def attend_row(row, carry):
        values = m.vt[row]
        parts = []
        for head in range(H):
            scores = m.at[row, head] * (INV_ROOT * LOG2E) + m.bias_t[head]
            top = jnp.max(scores, axis=0, keepdims=True)
            weights = jnp.exp2(scores - top)
            weights = weights * (1.0 / total(weights))
            m.at[row, head] = weights
            parts.append(dot(values[HD * head : HD * (head + 1)], weights.astype(BF16)))
        attended = jnp.concatenate(parts, axis=0)
        m.ot[row] = attended
        gated = (m.gt[row] * attended).astype(BF16)
        updated = m.zt[row] + dot(m.wo_t[...], gated) + m.obias_b[...]
        logits = dot(m.wd_t3[...], three(updated))
        m.lgt[row] = logits
        rounded = logits.astype(BF16)
        start = pl.multiple_of(L * row, L)
        m.lgn[pl.ds(start, L), :] = dot_nt(m.eye[...], jnp.concatenate([rounded, rounded], axis=0))
        return carry

    lax.fori_loop(0, R, attend_row, 0, unroll=True)

    order = [(1, d) for d in (4, 3, 5, 2, 6, 1, 7, 0)] + [(0, d) for d in (4, 3, 5, 2, 6, 1, 7, 0)]

    def peer_of(flip, step):
        return 8 * (half + flip * (1 - 2 * half)) + (place + step) % 8

    low_lanes = lax.broadcasted_iota(I32, (8, L), 1) < NB

    for index, (flip, step) in enumerate(order):
        dest = peer_of(flip, step)
        theirs = block_of(dest)
        parts = []
        for column_in in range(4):
            first = m.lgn[pl.ds(8 * theirs + column_in, 8, stride=L), :]
            second = m.lgn[pl.ds(8 * theirs + 4 + column_in, 8, stride=L), :]
            parts.append(jnp.where(low_lanes, first, second))
        m.c_stage[theirs] = jnp.concatenate(parts, axis=0).astype(BF16)
        if index < T - 1:
            pltpu.make_async_remote_copy(
                src_ref=m.c_stage.at[theirs],
                dst_ref=m.c_recv.at[block],
                send_sem=m.c_send.at[index],
                recv_sem=m.c_sem,
                device_id=(state, dest),
                device_id_type=MESH,
            ).start()
        else:
            pltpu.make_async_copy(m.c_stage.at[block], m.c_recv.at[block], m.c_sem).start()

    pltpu.make_async_copy(m.tg_recv, m.tg_recv, m.tg_sem).wait()
    pltpu.make_async_copy(m.c_recv, m.c_recv, m.c_sem).wait()

    received = [m.c_recv[peer].astype(F32) for peer in range(T)]
    for index in range(4):
        rows = jnp.concatenate([block[8 * index : 8 * (index + 1)] for block in received], axis=0)
        turned = jnp.transpose(rows)
        m.mirror[index] = turned[:NB]
        m.mirror[4 + index] = turned[NB:]

    bins = lax.broadcasted_iota(I32, (NB, L), 0)

    def backward_row(row, carry):
        logits = m.lgt[row] + m.mirror[row] + m.dbias_b[...]
        top = jnp.max(logits, axis=0, keepdims=True)
        expo = jnp.exp(logits - top)
        prob = expo * (1.0 / total(expo))
        wanted = m.tg_recv[row // 2, pl.ds(lax.rem(row, 2), 1), :]
        residual = prob - jnp.where(bins == wanted, 1.0, 0.0)
        pair_grad = dot(m.wd3[...], three(residual))
        m.dp[row] = pair_grad
        out_grad = dot(m.wo_v[...], pair_grad.astype(BF16))
        gate = m.gt[row]
        gated = out_grad * gate
        att_grad = gated.astype(BF16)
        m.dot[row] = att_grad
        m.dgt[row] = (gated * m.ot[row] * (1.0 - gate)).astype(BF16)
        values_n = m.vn[row]
        stacked = jnp.concatenate([values_n * m.hmask[head] for head in range(H)], axis=0)
        weight_grad = dot(stacked, att_grad)
        for head in range(H):
            span = slice(HD * head, HD * (head + 1))
            weights = m.at[row, head]
            grads = weight_grad[L * head : L * (head + 1)]
            score = weights * (grads - total(weights * grads))
            m.dbt[head] += score
            m.score_b[row, head] = score.astype(BF16)
        return carry

    lax.fori_loop(0, R, backward_row, 0, unroll=True)

    turned = [jnp.transpose(m.dbt[head]) for head in range(H)]
    for peer in range(T):
        m.e_stage[peer] = jnp.concatenate(
            [block[R * peer : R * (peer + 1)] for block in turned], axis=0
        ).astype(BF16)

    for index, (flip, step) in enumerate(order[:-1]):
        dest = peer_of(flip, step)
        pltpu.make_async_remote_copy(
            src_ref=m.e_stage.at[block_of(dest)],
            dst_ref=m.e_recv.at[block],
            send_sem=m.e_send.at[index],
            recv_sem=m.e_sem,
            device_id=(state, dest),
            device_id_type=MESH,
        ).start()
    pltpu.make_async_copy(m.e_stage.at[block], m.e_recv.at[block], m.e_sem).start()

    def back_project(row, carry):
        queries = m.qt[row]
        keys = m.kt[row]
        att_grad = m.dot[row]
        spans = [slice(HD * head, HD * (head + 1)) for head in range(H)]
        scores = [m.score_b[row, head] for head in range(H)]
        parts = [dot(keys[span], score) * INV_ROOT for span, score in zip(spans, scores)]
        parts += [dot_nt(queries[span], score) * INV_ROOT for span, score in zip(spans, scores)]
        parts += [dot_nt(att_grad[span], m.at[row, head].astype(BF16)) for head, span in enumerate(spans)]
        grads = jnp.concatenate(parts, axis=0).astype(BF16)
        m.zt[row] = dot(m.w_in[...], jnp.concatenate([grads, m.dgt[row]], axis=0))
        return carry

    lax.fori_loop(0, R, back_project, 0, unroll=True)

    pltpu.make_async_copy(m.e_recv, m.e_recv, m.e_sem).wait()
    bias_sum = m.e_recv[0].astype(F32)
    for peer in range(1, T):
        bias_sum = bias_sum + m.e_recv[peer].astype(F32)
    m.dbs[...] = bias_sum

    def finish_pair(pair, carry):
        for side in range(2):
            row = 2 * pair + side
            zn_grad = m.zt[row]
            for head in range(H):
                zn_grad = zn_grad + m.wpb_b[head] * m.dbs[pl.ds(R * head + row, 1), :]
            scaled = zn_grad * m.gain_b[...]
            normed = m.xh[row]
            mean = total(scaled) * (1.0 / C)
            slope = total(scaled * normed) * (1.0 / C)
            result = m.dp[row] + m.inv[row] * (scaled - mean - normed * slope)
            m.grad[row] = dot_nt(m.shift[...], result.astype(BF16))

        target = 4 * group + pair
        for step, (dy, dz) in enumerate(state_order):
            dest = 4 * lax.rem(state // 4 + dy, 4) + lax.rem(state % 4 + dz, 4)
            start = pl.multiple_of(8 * dest, 8)
            upper = m.grad[2 * pair, pl.ds(start, 8), :]
            lower = m.grad[2 * pair + 1, pl.ds(start, 8), :]
            m.f_stage[pair, dest] = jnp.concatenate([upper, lower], axis=0).astype(BF16)

            def send(dest=dest, step=step):
                pltpu.make_async_remote_copy(
                    src_ref=m.f_stage.at[pair, dest],
                    dst_ref=m.f_recv.at[state, band],
                    send_sem=m.f_send.at[pair, step],
                    recv_sem=m.f_sem,
                    device_id=(dest, target),
                    device_id_type=MESH,
                ).start()

            if step < S - 1:
                send()
            else:
                pl.when(target != tile)(send)

                @pl.when(target == tile)
                def _():
                    pltpu.make_async_copy(
                        m.f_stage.at[pair, state], m.f_recv.at[state, band], m.f_sem
                    ).start()

        return carry

    state_order = [(dy, dz) for dy in (2, 1, 3, 0) for dz in (2, 1, 3, 0)]
    lax.fori_loop(0, 4, finish_pair, 0, unroll=True)

    for step in (2, 3, 1):
        tile_copy(step).wait_send()
    for index in range(4):

        @pl.when(4 * index + swap(band) != tile)
        def _():
            pltpu.make_async_copy(m.tg_stage.at[0], m.tg_stage.at[0], m.tg_send.at[index]).wait()

    for index in range(15):
        pltpu.make_async_copy(m.b_stage, m.b_stage, m.b_send.at[index]).wait()

    def sent(step, carry):
        pltpu.make_async_copy(m.c_stage.at[0], m.c_stage.at[0], m.c_send.at[step]).wait()
        pltpu.make_async_copy(m.e_stage.at[0], m.e_stage.at[0], m.e_send.at[step]).wait()
        return carry

    lax.fori_loop(0, T - 1, sent, 0)

    pltpu.make_async_copy(m.f_recv, m.f_recv, m.f_sem).wait()
    out[...] = dot(m.spread[...], m.f_recv[...].reshape(S * 64, C)).reshape(out.shape)

    def sent_state(step, carry):
        for pair in range(4):

            @pl.when(jnp.logical_or(step < S - 1, 4 * group + pair != tile))
            def _():
                pltpu.make_async_copy(
                    m.f_stage.at[0, 0], m.f_stage.at[0, 0], m.f_send.at[pair, step]
                ).wait()

        return carry

    lax.fori_loop(0, S, sent_state, 0)


def on_device(
    pair_tiles,
    targets,
    offsets,
    ln_gain,
    ln_bias,
    w_query,
    w_key,
    w_value,
    w_pairbias,
    w_gate,
    gate_bias,
    w_output,
    out_bias,
    w_distogram,
    dist_bias,
):
    anywhere = pl.BlockSpec(memory_space=pltpu.HBM)
    in_specs = [anywhere] * 15
    in_specs[2] = pl.BlockSpec(memory_space=pltpu.SMEM)
    return pl.pallas_call(
        kernel,
        out_shape=jax.ShapeDtypeStruct((8, 1, 2, 2, L // S, C), F32),
        in_specs=in_specs,
        out_specs=pl.BlockSpec(memory_space=pltpu.VMEM),
        scratch_shapes=list(SCRATCH.values()),
        compiler_params=pltpu.CompilerParams(
            collective_id=0, has_side_effects=True, vmem_limit_bytes=64 * 1024 * 1024
        ),
    )(
        pair_tiles,
        targets,
        offsets,
        ln_gain.reshape(1, C),
        ln_bias.reshape(1, C),
        w_query,
        w_key,
        w_value,
        w_pairbias.T,
        w_gate,
        gate_bias.reshape(1, C),
        w_output,
        out_bias.reshape(1, C),
        w_distogram.T,
        dist_bias.reshape(1, NB),
    )


def solution(mesh):
    in_specs = (
        P("state", "tile", None, None, None),
        P("state", "tile", None, None, None),
    ) + (P(),) * 13
    out_specs = P(None, "tile", None, None, "state", None)
    return jax.shard_map(
        on_device, mesh=mesh, in_specs=in_specs, out_specs=out_specs, check_vma=False
    )
```

```python
import math

import jax
import jax.numpy as jnp
from jax import lax
from jax.experimental import pallas as pl
from jax.experimental.pallas import tpu as pltpu
from jax.sharding import PartitionSpec as P

C = 128
H = 4
HD = 32
NB = 64
L = 128
S = 16
T = 16
R = 8
F32 = jnp.float32
BF16 = jnp.bfloat16
I32 = jnp.int32
MESH = pl.DeviceIdType.MESH
LOG2E = 1.0 / math.log(2.0)
INV_ROOT = 1.0 / math.sqrt(HD)

SCRATCH = dict(
    gain_v=pltpu.VMEM((1, C), F32),
    lbias_v=pltpu.VMEM((1, C), F32),
    wq_v=pltpu.VMEM((C, C), BF16),
    wk_v=pltpu.VMEM((C, C), BF16),
    wv_v=pltpu.VMEM((C, C), BF16),
    wg_v=pltpu.VMEM((C, C), BF16),
    wo_v=pltpu.VMEM((C, C), BF16),
    wpb_v=pltpu.VMEM((H, C), F32),
    gbias_v=pltpu.VMEM((1, C), F32),
    obias_v=pltpu.VMEM((1, C), F32),
    wd_v=pltpu.VMEM((NB, C), F32),
    dbias_v=pltpu.VMEM((1, NB), F32),
    targets_v=pltpu.VMEM((2, 4, L), I32),
    w_sem=pltpu.SemaphoreType.DMA((14,)),
    eye=pltpu.VMEM((C, C), BF16),
    hmask=pltpu.VMEM((H, C, C), BF16),
    shift=pltpu.VMEM((L, L), BF16),
    spread=pltpu.VMEM((256, S * 64), BF16),
    w_in_t=pltpu.VMEM((4 * C, C), BF16),
    w_in=pltpu.VMEM((C, 4 * C), BF16),
    wo_t=pltpu.VMEM((C, C), BF16),
    wd_t3=pltpu.VMEM((NB, 3 * C), BF16),
    wd3=pltpu.VMEM((C, 3 * NB), BF16),
    gain_b=pltpu.VMEM((C, L), F32),
    lbias_b=pltpu.VMEM((C, L), F32),
    gbias_b=pltpu.VMEM((C, L), F32),
    obias_b=pltpu.VMEM((C, L), F32),
    dbias_b=pltpu.VMEM((NB, L), F32),
    wpb_b=pltpu.VMEM((H, C, L), F32),
    zb=pltpu.VMEM((R, L, C), BF16),
    zt=pltpu.VMEM((R, C, L), F32),
    xh=pltpu.VMEM((R, C, L), F32),
    inv=pltpu.VMEM((R, 1, L), F32),
    znb=pltpu.VMEM((R, C, L), BF16),
    qt=pltpu.VMEM((R, C, L), BF16),
    kt=pltpu.VMEM((R, C, L), BF16),
    vt=pltpu.VMEM((R, C, L), BF16),
    vn=pltpu.VMEM((R, L, C), BF16),
    gt=pltpu.VMEM((R, C, L), F32),
    ot=pltpu.VMEM((R, C, L), F32),
    at=pltpu.VMEM((R, H, L, L), F32),
    bias_t=pltpu.VMEM((H, L, L), F32),
    lgt=pltpu.VMEM((R, NB, L), F32),
    lgn=pltpu.VMEM((R * L, C), F32),
    mirror=pltpu.VMEM((R, NB, L), F32),
    dp=pltpu.VMEM((R, C, L), F32),
    dgt=pltpu.VMEM((R, C, L), BF16),
    dot=pltpu.VMEM((R, C, L), BF16),
    score_b=pltpu.VMEM((R, H, L, L), BF16),
    dbt=pltpu.VMEM((H, L, L), F32),
    dbs=pltpu.VMEM((H * R, L), F32),
    grad=pltpu.VMEM((R, L, C), F32),
    tg_stage=pltpu.VMEM((4, 8, L), I32),
    tg_recv=pltpu.VMEM((4, 8, L), I32),
    tile_v=pltpu.VMEM((32, 32, C), BF16),
    b_rows=pltpu.VMEM((H * R, L), F32),
    b_stage=pltpu.VMEM((32, L), F32),
    b_recv=pltpu.VMEM((T, 32, L), F32),
    c_stage=pltpu.VMEM((T, 32, L), BF16),
    c_recv=pltpu.VMEM((T, 32, L), BF16),
    e_stage=pltpu.VMEM((T, 32, L), BF16),
    e_recv=pltpu.VMEM((T, 32, L), BF16),
    f_stage=pltpu.VMEM((4, S, 16, C), BF16),
    f_recv=pltpu.VMEM((S, 4, 16, C), BF16),
    a_send=pltpu.SemaphoreType.DMA((4,)),
    a_sem=pltpu.SemaphoreType.DMA,
    tg_send=pltpu.SemaphoreType.DMA((4,)),
    tg_sem=pltpu.SemaphoreType.DMA,
    b_send=pltpu.SemaphoreType.DMA((16,)),
    b_sem=pltpu.SemaphoreType.DMA((3,)),
    c_send=pltpu.SemaphoreType.DMA((T,)),
    c_sem=pltpu.SemaphoreType.DMA,
    e_send=pltpu.SemaphoreType.DMA((T,)),
    e_sem=pltpu.SemaphoreType.DMA,
    f_send=pltpu.SemaphoreType.DMA((4, S)),
    f_sem=pltpu.SemaphoreType.DMA,
)
NAMES = tuple(SCRATCH)


class Refs:
    pass


def dot(left, right):
    return jnp.dot(left, right, preferred_element_type=F32)


def dot_nt(left, right):
    return lax.dot_general(left, right, (((1,), (1,)), ((), ())), preferred_element_type=F32)


def halves(values):
    high = values.astype(BF16)
    low = (values - high.astype(F32)).astype(BF16)
    return high, low


def three(values):
    high, low = halves(values)
    return jnp.concatenate([high, low, high], axis=0)


def total(values):
    return jnp.sum(values, axis=0, keepdims=True)


def swap(index):
    return 2 * (index % 2) + index // 2


def block_of(device):
    return device - device % 4 + swap(device % 4)


def column(row):
    width = row.shape[1]
    return jnp.transpose(jnp.broadcast_to(row, (L, width)))


def kernel(
    tiles,
    targets,
    offsets,
    gain,
    lbias,
    wq,
    wk,
    wv,
    wpb,
    wg,
    gbias,
    wo,
    obias,
    wd,
    dbias,
    out,
    *scratch,
):
    m = Refs()
    for name, ref in zip(NAMES, scratch):
        setattr(m, name, ref)
    state = lax.axis_index("state")
    tile = lax.axis_index("tile")
    band = tile // 4
    sub = tile % 4
    group = swap(sub)
    block = 4 * band + group

    barrier = pltpu.get_barrier_semaphore()

    def greet_tile(step, carry):
        peer = lax.rem(tile + step, T)
        pl.semaphore_signal(barrier, inc=1, device_id=(state, peer), device_id_type=MESH)
        return carry

    lax.fori_loop(1, T, greet_tile, 0)

    def greet_state(step, carry):
        peer = lax.rem(state + step, S)
        for index in range(4):
            pl.semaphore_signal(
                barrier, inc=1, device_id=(peer, 4 * index + swap(band)), device_id_type=MESH
            )
        return carry

    lax.fori_loop(1, S, greet_state, 0)

    loads = []
    for index, (source, target) in enumerate(
        [
            (gain, m.gain_v),
            (lbias, m.lbias_v),
            (wq, m.wq_v),
            (wk, m.wk_v),
            (wv, m.wv_v),
            (wg, m.wg_v),
            (wo, m.wo_v),
            (wpb, m.wpb_v),
            (gbias, m.gbias_v),
            (obias, m.obias_v),
            (wd, m.wd_v),
            (dbias, m.dbias_v),
            (targets.at[0, 0], m.targets_v),
            (tiles.at[0, 0], m.tile_v),
        ]
    ):
        load = pltpu.make_async_copy(source, target, m.w_sem.at[index])
        load.start()
        loads.append(load)

    rows_i = lax.broadcasted_iota(I32, (C, C), 0)
    cols_i = lax.broadcasted_iota(I32, (C, C), 1)
    m.eye[...] = jnp.where(rows_i == cols_i, 1.0, 0.0).astype(BF16)
    for head in range(H):
        m.hmask[head] = jnp.where(cols_i // HD == head, 1.0, 0.0).astype(BF16)
    early = (0, 1, 7, 13)
    late_loads = [load for index, load in enumerate(loads) if index not in early]
    for index in early:
        loads[index].wait()
    eye = m.eye[...]
    m.gain_b[...] = column(m.gain_v[...])
    m.lbias_b[...] = column(m.lbias_v[...])
    for head in range(H):
        m.wpb_b[head] = column(m.wpb_v[head : head + 1])

    for index in range(R):
        z = dot_nt(eye, m.tile_v[4 * index : 4 * (index + 1)].reshape(L, C))
        centre = z - total(z) * (1.0 / C)
        inverse = lax.rsqrt(total(centre * centre) * (1.0 / C) + 1e-05)
        zn = centre * inverse * m.gain_b[...] + m.lbias_b[...]
        for head in range(H):
            m.b_rows[R * head + index : R * head + index + 1, :] = total(zn * m.wpb_b[head]) * LOG2E
    turned = jnp.transpose(m.b_rows[...])
    rows_s = lax.broadcasted_iota(I32, (32, L), 0)
    cols_s = lax.broadcasted_iota(I32, (32, L), 1)
    tile_bias = jnp.zeros((32, L), F32)
    for part in range(3):
        piece = turned.astype(BF16)
        turned = turned - piece.astype(F32)
        for index in range(4):
            lane = 32 * (rows_s // R) + 4 * (rows_s % R) + index
            place_it = jnp.where(lane == cols_s, 1.0, 0.0).astype(BF16)
            tile_bias = tile_bias + dot(piece[32 * index : 32 * (index + 1)], place_it)
    m.b_stage[...] = tile_bias

    pl.semaphore_wait(barrier, T - 1 + 4 * (S - 1))

    def tile_copy(step):
        other = lax.rem(sub + step, 4)
        return pltpu.make_async_remote_copy(
            src_ref=tiles.at[0, 0, pl.ds(R * swap(other), R)],
            dst_ref=m.zb.at[:, pl.ds(pl.multiple_of(32 * sub, 32), 32), :],
            send_sem=m.a_send.at[step],
            recv_sem=m.a_sem,
            device_id=(state, 4 * band + other),
            device_id_type=MESH,
        )

    half = tile // 8
    place = tile % 8
    partner = 8 * (1 - half) + place

    def bias_copy(source, slot, index, sem, dest):
        return pltpu.make_async_remote_copy(
            src_ref=source,
            dst_ref=m.b_recv.at[slot],
            send_sem=m.b_send.at[index],
            recv_sem=m.b_sem.at[sem],
            device_id=(state, dest),
            device_id_type=MESH,
        )

    bias_copy(m.b_stage, tile, 0, 0, partner).start()
    for step in (2, 3, 1):
        tile_copy(step).start()
    pltpu.make_async_copy(
        tiles.at[0, 0, pl.ds(R * group, R)],
        m.zb.at[:, pl.ds(pl.multiple_of(32 * sub, 32), 32), :],
        m.a_sem,
    ).start()
    for step in range(1, 8):
        dest = 8 * half + (place + step) % 8
        bias_copy(m.b_stage, tile, step, 1, dest).start()
    pltpu.make_async_copy(m.b_stage, m.b_recv.at[tile], m.b_sem.at[1]).start()

    m.shift[...] = jnp.where(((rows_i - offsets[state] + L) & (L - 1)) == cols_i, 1.0, 0.0).astype(BF16)
    rows_o = lax.broadcasted_iota(I32, (256, L), 0)
    cols_o = lax.broadcasted_iota(I32, (256, L), 1)
    row_in = 8 * ((rows_o >> 4) & 1) + (rows_o & 7)
    same_row = row_in == (cols_o & 15)
    band_gap = 32 * ((rows_o >> 5) - ((cols_o >> 4) & 3))
    upper_half = (rows_o >> 3) & 1
    for index in range(S // 2):
        offset = jnp.where(cols_o < 64, offsets[2 * index], offsets[2 * index + 1])
        wrapped = jnp.where(offset > 8 * state, 1, 0)
        chosen = same_row & (band_gap == offset) & (upper_half == wrapped)
        m.spread[:, L * index : L * (index + 1)] = jnp.where(chosen, 1.0, 0.0).astype(BF16)
    for load in late_loads:
        load.wait()
    for index in range(4):
        m.tg_stage[index] = jnp.concatenate([m.targets_v[:, index, :]] * 4, axis=0)
    for index in range(4):
        dest = 4 * index + swap(band)

        @pl.when(dest != tile)
        def _():
            pltpu.make_async_remote_copy(
                src_ref=m.tg_stage.at[index],
                dst_ref=m.tg_recv.at[sub],
                send_sem=m.tg_send.at[index],
                recv_sem=m.tg_sem,
                device_id=(state, dest),
                device_id_type=MESH,
            ).start()

        @pl.when(dest == tile)
        def _():
            pltpu.make_async_copy(m.tg_stage.at[index], m.tg_recv.at[sub], m.tg_sem).start()

    for index, ref in enumerate((m.wq_v, m.wk_v, m.wv_v, m.wg_v)):
        weight = ref[...]
        m.w_in[:, C * index : C * (index + 1)] = weight
        m.w_in_t[C * index : C * (index + 1), :] = dot_nt(eye, weight).astype(BF16)
    m.wo_t[...] = dot_nt(eye, m.wo_v[...]).astype(BF16)
    head_w = m.wd_v[...]
    high, low = halves(2.0 * jnp.transpose(head_w))
    m.wd3[...] = jnp.concatenate([high, high, low], axis=1)
    high, low = halves(head_w - total(head_w) * (1.0 / NB))
    m.wd_t3[...] = jnp.concatenate([high, high, low], axis=1)
    m.gbias_b[...] = column(m.gbias_v[...])
    m.obias_b[...] = column(m.obias_v[...])
    m.dbias_b[...] = column(m.dbias_v[...])
    m.dbt[...] = jnp.zeros_like(m.dbt)

    pltpu.make_async_copy(m.zb, m.zb, m.a_sem).wait()

    def norm_row(row, carry):
        z = dot_nt(m.eye[...], m.zb[row])
        centre = z - total(z) * (1.0 / C)
        inverse = lax.rsqrt(total(centre * centre) * (1.0 / C) + 1e-05)
        normed = centre * inverse
        zn = normed * m.gain_b[...] + m.lbias_b[...]
        m.zt[row] = z
        m.xh[row] = normed
        m.inv[row] = inverse
        m.znb[row] = zn.astype(BF16)
        return carry

    lax.fori_loop(0, R, norm_row, 0, unroll=True)

    pltpu.make_async_copy(m.b_stage, m.b_recv.at[partner], m.b_sem.at[0]).wait()
    for step in range(1, 8):
        dest = 8 * half + (place + step) % 8
        bias_copy(m.b_recv.at[partner], partner, 7 + step, 2, dest).start()

    for row in range(0, R, 2):
        proj = dot(m.w_in_t[...], jnp.concatenate([m.znb[row], m.znb[row + 1]], axis=1))
        queries_keys_values = proj[: 3 * C].astype(BF16)
        gates = proj[3 * C :]
        for side in range(2):
            here = row + side
            span = slice(L * side, L * (side + 1))
            m.qt[here] = queries_keys_values[:C, span]
            m.kt[here] = queries_keys_values[C : 2 * C, span]
            m.vt[here] = queries_keys_values[2 * C :, span]
            m.gt[here] = jax.nn.sigmoid(gates[:, span] + m.gbias_b[...])
            natural = dot_nt(m.eye[...], queries_keys_values[C:, span]).astype(BF16)
            m.vn[here] = natural[:, C:]
            stacked = jnp.concatenate([natural[:, :C] * m.hmask[head] for head in range(H)], axis=0)
            scores = dot(stacked, queries_keys_values[:C, span]) * (INV_ROOT * LOG2E)
            m.at[here] = scores.reshape(H, L, L)

    pltpu.make_async_copy(m.b_recv.at[pl.ds(0, 8)], m.b_recv.at[pl.ds(0, 8)], m.b_sem.at[1]).wait()
    pltpu.make_async_copy(m.b_recv.at[pl.ds(0, 7)], m.b_recv.at[pl.ds(0, 7)], m.b_sem.at[2]).wait()
    bands = [m.b_recv[4 * index : 4 * (index + 1)].reshape(L, L) for index in range(4)]
    for head in range(H):
        m.bias_t[head] = jnp.concatenate([part[:, 32 * head : 32 * (head + 1)] for part in bands], axis=1)

    def attend(row):
        values = m.vt[row]
        parts = []
        for head in range(H):
            scores = m.at[row, head] + m.bias_t[head]
            top = jnp.max(scores, axis=0, keepdims=True)
            weights = jnp.exp2(scores - top)
            weights = weights * (1.0 / total(weights))
            m.at[row, head] = weights
            parts.append(dot(values[HD * head : HD * (head + 1)], weights.astype(BF16)))
        attended = jnp.concatenate(parts, axis=0)
        m.ot[row] = attended
        return (m.gt[row] * attended).astype(BF16)

    def predict(row, gated):
        added = dot(m.wo_t[...], jnp.concatenate(gated, axis=1))
        updated = jnp.concatenate([m.zt[row] + m.obias_b[...], m.zt[row + 1] + m.obias_b[...]], axis=1) + added
        logits = dot(m.wd_t3[...], three(updated))
        m.lgt[row] = logits[:, :L]
        m.lgt[row + 1] = logits[:, L:]
        rounded = logits.astype(BF16)
        first, second = rounded[:, :L], rounded[:, L:]
        turned = dot_nt(m.eye[...], jnp.concatenate([first, first, second, second], axis=0))
        m.lgn[L * row : L * (row + 1), :] = turned[:, :C]
        m.lgn[L * (row + 1) : L * (row + 2), :] = turned[:, C:]

    waiting = None
    for row in range(0, R, 2):
        gated = [attend(row), attend(row + 1)]
        if waiting is not None:
            predict(*waiting)
        waiting = (row, gated)
    predict(*waiting)

    order = [(1, d) for d in (4, 3, 5, 2, 6, 1, 7, 0)] + [(0, d) for d in (4, 3, 5, 2, 6, 1, 7, 0)]

    def peer_of(flip, step):
        return 8 * (half + flip * (1 - 2 * half)) + (place + step) % 8

    low_lanes = lax.broadcasted_iota(I32, (8, L), 1) < NB

    for index, (flip, step) in enumerate(order):
        dest = peer_of(flip, step)
        theirs = block_of(dest)
        parts = []
        for column_in in range(4):
            first = m.lgn[pl.ds(8 * theirs + column_in, 8, stride=L), :]
            second = m.lgn[pl.ds(8 * theirs + 4 + column_in, 8, stride=L), :]
            parts.append(jnp.where(low_lanes, first, second))
        m.c_stage[theirs] = jnp.concatenate(parts, axis=0).astype(BF16)
        if index < T - 1:
            pltpu.make_async_remote_copy(
                src_ref=m.c_stage.at[theirs],
                dst_ref=m.c_recv.at[block],
                send_sem=m.c_send.at[index],
                recv_sem=m.c_sem,
                device_id=(state, dest),
                device_id_type=MESH,
            ).start()
        else:
            pltpu.make_async_copy(m.c_stage.at[block], m.c_recv.at[block], m.c_sem).start()

    pltpu.make_async_copy(m.tg_recv, m.tg_recv, m.tg_sem).wait()
    pltpu.make_async_copy(m.c_recv, m.c_recv, m.c_sem).wait()

    received = [m.c_recv[peer].astype(F32) for peer in range(T)]
    for index in range(4):
        rows = jnp.concatenate([block[8 * index : 8 * (index + 1)] for block in received], axis=0)
        turned = jnp.transpose(rows)
        m.mirror[index] = turned[:NB]
        m.mirror[4 + index] = turned[NB:]

    bins = lax.broadcasted_iota(I32, (NB, L), 0)

    def residual(row):
        logits = m.lgt[row] + m.mirror[row] + m.dbias_b[...]
        top = jnp.max(logits, axis=0, keepdims=True)
        expo = jnp.exp(logits - top)
        prob = expo * (1.0 / total(expo))
        wanted = m.tg_recv[row // 2, row % 2 : row % 2 + 1, :]
        return prob - jnp.where(bins == wanted, 1.0, 0.0)

    def out_gradient(row):
        pair_grad = dot(m.wd3[...], three(jnp.concatenate([residual(row), residual(row + 1)], axis=1)))
        m.dp[row] = pair_grad[:, :L]
        m.dp[row + 1] = pair_grad[:, L:]
        return dot(m.wo_v[...], pair_grad.astype(BF16))

    def score_gradient(row, out_grad):
        gate = m.gt[row]
        gated = out_grad * gate
        att_grad = gated.astype(BF16)
        m.dot[row] = att_grad
        m.dgt[row] = (gated * m.ot[row] * (1.0 - gate)).astype(BF16)
        values_n = m.vn[row]
        stacked = jnp.concatenate([values_n * m.hmask[head] for head in range(H)], axis=0)
        weight_grad = dot(stacked, att_grad)
        for head in range(H):
            weights = m.at[row, head]
            grads = weight_grad[L * head : L * (head + 1)]
            score = weights * (grads - total(weights * grads))
            m.dbt[head] += score
            m.score_b[row, head] = score.astype(BF16)

    grads = out_gradient(0)
    for row in range(0, R, 2):
        current = grads
        if row + 2 < R:
            grads = out_gradient(row + 2)
        score_gradient(row, current[:, :L])
        score_gradient(row + 1, current[:, L:])

    turned = [jnp.transpose(m.dbt[head]) for head in range(H)]
    for peer in range(T):
        m.e_stage[peer] = jnp.concatenate(
            [block[R * peer : R * (peer + 1)] for block in turned], axis=0
        ).astype(BF16)

    for index, (flip, step) in enumerate(order[:-1]):
        dest = peer_of(flip, step)
        pltpu.make_async_remote_copy(
            src_ref=m.e_stage.at[block_of(dest)],
            dst_ref=m.e_recv.at[block],
            send_sem=m.e_send.at[index],
            recv_sem=m.e_sem,
            device_id=(state, dest),
            device_id_type=MESH,
        ).start()
    pltpu.make_async_copy(m.e_stage.at[block], m.e_recv.at[block], m.e_sem).start()

    def projections(row):
        queries = m.qt[row]
        keys = m.kt[row]
        att_grad = m.dot[row]
        spans = [slice(HD * head, HD * (head + 1)) for head in range(H)]
        scores = [m.score_b[row, head] for head in range(H)]
        parts = [dot(keys[span], score) * INV_ROOT for span, score in zip(spans, scores)]
        parts += [dot_nt(queries[span], score) * INV_ROOT for span, score in zip(spans, scores)]
        parts += [dot_nt(att_grad[span], m.at[row, head].astype(BF16)) for head, span in enumerate(spans)]
        return jnp.concatenate([jnp.concatenate(parts, axis=0).astype(BF16), m.dgt[row]], axis=0)

    for row in range(0, R, 2):
        both = dot(m.w_in[...], jnp.concatenate([projections(row), projections(row + 1)], axis=1))
        m.zt[row] = both[:, :L]
        m.zt[row + 1] = both[:, L:]

    pltpu.make_async_copy(m.e_recv, m.e_recv, m.e_sem).wait()
    bias_sum = m.e_recv[0].astype(F32)
    for peer in range(1, T):
        bias_sum = bias_sum + m.e_recv[peer].astype(F32)
    m.dbs[...] = bias_sum

    def finish_pair(pair, carry):
        for side in range(2):
            row = 2 * pair + side
            zn_grad = m.zt[row]
            for head in range(H):
                zn_grad = zn_grad + m.wpb_b[head] * m.dbs[pl.ds(R * head + row, 1), :]
            scaled = zn_grad * m.gain_b[...]
            normed = m.xh[row]
            mean = total(scaled) * (1.0 / C)
            slope = total(scaled * normed) * (1.0 / C)
            result = m.dp[row] + m.inv[row] * (scaled - mean - normed * slope)
            m.grad[row] = dot_nt(m.shift[...], result.astype(BF16))

        target = 4 * group + pair
        for step, (dy, dz) in enumerate(state_order):
            dest = 4 * lax.rem(state // 4 + dy, 4) + lax.rem(state % 4 + dz, 4)
            start = pl.multiple_of(8 * dest, 8)
            upper = m.grad[2 * pair, pl.ds(start, 8), :]
            lower = m.grad[2 * pair + 1, pl.ds(start, 8), :]
            m.f_stage[pair, dest] = jnp.concatenate([upper, lower], axis=0).astype(BF16)

            def send(dest=dest, step=step):
                pltpu.make_async_remote_copy(
                    src_ref=m.f_stage.at[pair, dest],
                    dst_ref=m.f_recv.at[state, band],
                    send_sem=m.f_send.at[pair, step],
                    recv_sem=m.f_sem,
                    device_id=(dest, target),
                    device_id_type=MESH,
                ).start()

            if step < S - 1:
                send()
            else:
                pl.when(target != tile)(send)

                @pl.when(target == tile)
                def _():
                    pltpu.make_async_copy(
                        m.f_stage.at[pair, state], m.f_recv.at[state, band], m.f_sem
                    ).start()

        return carry

    state_order = [(dy, dz) for dy in (2, 1, 3, 0) for dz in (2, 1, 3, 0)]
    lax.fori_loop(0, 4, finish_pair, 0, unroll=True)

    for step in (2, 3, 1):
        tile_copy(step).wait_send()
    for index in range(4):

        @pl.when(4 * index + swap(band) != tile)
        def _():
            pltpu.make_async_copy(m.tg_stage.at[0], m.tg_stage.at[0], m.tg_send.at[index]).wait()

    for index in range(15):
        pltpu.make_async_copy(m.b_stage, m.b_stage, m.b_send.at[index]).wait()

    def sent(step, carry):
        pltpu.make_async_copy(m.c_stage.at[0], m.c_stage.at[0], m.c_send.at[step]).wait()
        pltpu.make_async_copy(m.e_stage.at[0], m.e_stage.at[0], m.e_send.at[step]).wait()
        return carry

    lax.fori_loop(0, T - 1, sent, 0)

    pltpu.make_async_copy(m.f_recv, m.f_recv, m.f_sem).wait()
    out[...] = dot(m.spread[...], m.f_recv[...].reshape(S * 64, C)).reshape(out.shape)

    def sent_state(step, carry):
        for pair in range(4):

            @pl.when(jnp.logical_or(step < S - 1, 4 * group + pair != tile))
            def _():
                pltpu.make_async_copy(
                    m.f_stage.at[0, 0], m.f_stage.at[0, 0], m.f_send.at[pair, step]
                ).wait()

        return carry

    lax.fori_loop(0, S, sent_state, 0)


def on_device(
    pair_tiles,
    targets,
    offsets,
    ln_gain,
    ln_bias,
    w_query,
    w_key,
    w_value,
    w_pairbias,
    w_gate,
    gate_bias,
    w_output,
    out_bias,
    w_distogram,
    dist_bias,
):
    anywhere = pl.BlockSpec(memory_space=pltpu.HBM)
    in_specs = [anywhere] * 15
    in_specs[2] = pl.BlockSpec(memory_space=pltpu.SMEM)
    return pl.pallas_call(
        kernel,
        out_shape=jax.ShapeDtypeStruct((8, 1, 2, 2, L // S, C), F32),
        in_specs=in_specs,
        out_specs=pl.BlockSpec(memory_space=pltpu.VMEM),
        scratch_shapes=list(SCRATCH.values()),
        compiler_params=pltpu.CompilerParams(
            collective_id=0, has_side_effects=True, vmem_limit_bytes=64 * 1024 * 1024
        ),
    )(
        pair_tiles,
        targets,
        offsets,
        ln_gain.reshape(1, C),
        ln_bias.reshape(1, C),
        w_query,
        w_key,
        w_value,
        w_pairbias.T,
        w_gate,
        gate_bias.reshape(1, C),
        w_output,
        out_bias.reshape(1, C),
        w_distogram.T,
        dist_bias.reshape(1, NB),
    )


def solution(mesh):
    in_specs = (
        P("state", "tile", None, None, None),
        P("state", "tile", None, None, None),
    ) + (P(),) * 13
    out_specs = P(None, "tile", None, None, "state", None)
    return jax.shard_map(
        on_device, mesh=mesh, in_specs=in_specs, out_specs=out_specs, check_vma=False
    )
```

```python
import math

import jax
import jax.numpy as jnp
from jax import lax
from jax.experimental import pallas as pl
from jax.experimental.pallas import tpu as pltpu
from jax.sharding import PartitionSpec as P

C = 128
H = 4
HD = 32
NB = 64
L = 128
S = 16
T = 16
R = 8
F32 = jnp.float32
BF16 = jnp.bfloat16
I32 = jnp.int32
MESH = pl.DeviceIdType.MESH
LOG2E = 1.0 / math.log(2.0)
INV_ROOT = 1.0 / math.sqrt(HD)

SCRATCH = dict(
    gain_v=pltpu.VMEM((1, C), F32),
    lbias_v=pltpu.VMEM((1, C), F32),
    wq_v=pltpu.VMEM((C, C), BF16),
    wk_v=pltpu.VMEM((C, C), BF16),
    wv_v=pltpu.VMEM((C, C), BF16),
    wg_v=pltpu.VMEM((C, C), BF16),
    wo_v=pltpu.VMEM((C, C), BF16),
    wpb_v=pltpu.VMEM((H, C), F32),
    gbias_v=pltpu.VMEM((1, C), F32),
    obias_v=pltpu.VMEM((1, C), F32),
    wd_v=pltpu.VMEM((NB, C), F32),
    dbias_v=pltpu.VMEM((1, NB), F32),
    targets_v=pltpu.VMEM((2, 4, L), I32),
    offsets_s=pltpu.SMEM((S,), I32),
    w_sem=pltpu.SemaphoreType.DMA((15,)),
    eye=pltpu.VMEM((C, C), BF16),
    hmask=pltpu.VMEM((H, C, C), BF16),
    shift=pltpu.VMEM((L, L), BF16),
    spread=pltpu.VMEM((256, S * 64), BF16),
    w_in_t=pltpu.VMEM((4 * C, C), BF16),
    w_in=pltpu.VMEM((C, 4 * C), BF16),
    wo_t=pltpu.VMEM((C, C), BF16),
    wd_t3=pltpu.VMEM((NB, 3 * C), BF16),
    wd3=pltpu.VMEM((C, 3 * NB), BF16),
    gain_b=pltpu.VMEM((C, L), F32),
    lbias_b=pltpu.VMEM((C, L), F32),
    gbias_b=pltpu.VMEM((C, L), F32),
    obias_b=pltpu.VMEM((C, L), F32),
    dbias_b=pltpu.VMEM((NB, L), F32),
    wpb_b=pltpu.VMEM((H, C, L), F32),
    zb=pltpu.VMEM((R, L, C), BF16),
    zt=pltpu.VMEM((R, C, L), F32),
    xh=pltpu.VMEM((R, C, L), F32),
    inv=pltpu.VMEM((R, 1, L), F32),
    znb=pltpu.VMEM((R, C, L), BF16),
    qt=pltpu.VMEM((R, C, L), BF16),
    kt=pltpu.VMEM((R, C, L), BF16),
    vt=pltpu.VMEM((R, C, L), BF16),
    vn=pltpu.VMEM((R, L, C), BF16),
    gt=pltpu.VMEM((R, C, L), F32),
    ot=pltpu.VMEM((R, C, L), F32),
    at=pltpu.VMEM((R, H, L, L), F32),
    bias_t=pltpu.VMEM((H, L, L), F32),
    lgt=pltpu.VMEM((R, NB, L), F32),
    lgn=pltpu.VMEM((R * L, C), F32),
    mirror=pltpu.VMEM((R, NB, L), F32),
    dp=pltpu.VMEM((R, C, L), F32),
    dgt=pltpu.VMEM((R, C, L), BF16),
    dot=pltpu.VMEM((R, C, L), BF16),
    score_b=pltpu.VMEM((R, H, L, L), BF16),
    dbt=pltpu.VMEM((H, L, L), F32),
    dbs=pltpu.VMEM((H * R, L), F32),
    grad=pltpu.VMEM((R, L, C), F32),
    tg_stage=pltpu.VMEM((4, 8, L), I32),
    tg_recv=pltpu.VMEM((4, 8, L), I32),
    tile_v=pltpu.VMEM((32, 32, C), BF16),
    b_rows=pltpu.VMEM((H * R, L), F32),
    b_stage=pltpu.VMEM((32, L), F32),
    b_recv=pltpu.VMEM((T, 32, L), F32),
    c_stage=pltpu.VMEM((T, 32, L), BF16),
    c_recv=pltpu.VMEM((T, 32, L), BF16),
    e_stage=pltpu.VMEM((T, 32, L), BF16),
    e_recv=pltpu.VMEM((T, 32, L), BF16),
    f_stage=pltpu.VMEM((4, S, 16, C), BF16),
    f_recv=pltpu.VMEM((S, 4, 16, C), BF16),
    a_send=pltpu.SemaphoreType.DMA((4,)),
    a_sem=pltpu.SemaphoreType.DMA,
    tg_send=pltpu.SemaphoreType.DMA((4,)),
    tg_sem=pltpu.SemaphoreType.DMA,
    b_send=pltpu.SemaphoreType.DMA((16,)),
    b_sem=pltpu.SemaphoreType.DMA((3,)),
    c_send=pltpu.SemaphoreType.DMA((T,)),
    c_sem=pltpu.SemaphoreType.DMA,
    e_send=pltpu.SemaphoreType.DMA((T,)),
    e_sem=pltpu.SemaphoreType.DMA,
    f_send=pltpu.SemaphoreType.DMA((4, S)),
    f_sem=pltpu.SemaphoreType.DMA,
)
NAMES = tuple(SCRATCH)


class Refs:
    pass


def dot(left, right):
    return jnp.dot(left, right, preferred_element_type=F32)


def dot_nt(left, right):
    return lax.dot_general(left, right, (((1,), (1,)), ((), ())), preferred_element_type=F32)


def halves(values):
    high = values.astype(BF16)
    low = (values - high.astype(F32)).astype(BF16)
    return high, low


def three(values):
    high, low = halves(values)
    return jnp.concatenate([high, low, high], axis=0)


def total(values):
    return jnp.sum(values, axis=0, keepdims=True)


def swap(index):
    return 2 * (index % 2) + index // 2


def block_of(device):
    return device - device % 4 + swap(device % 4)


def column(row):
    width = row.shape[1]
    return jnp.transpose(jnp.broadcast_to(row, (L, width)))


def kernel(
    tiles,
    targets,
    offsets,
    gain,
    lbias,
    wq,
    wk,
    wv,
    wpb,
    wg,
    gbias,
    wo,
    obias,
    wd,
    dbias,
    out,
    *scratch,
):
    m = Refs()
    for name, ref in zip(NAMES, scratch):
        setattr(m, name, ref)
    state = lax.axis_index("state")
    tile = lax.axis_index("tile")
    band = tile // 4
    sub = tile % 4
    group = swap(sub)
    block = 4 * band + group

    barrier = pltpu.get_barrier_semaphore()

    def greet_tile(step, carry):
        peer = lax.rem(tile + step, T)
        pl.semaphore_signal(barrier, inc=1, device_id=(state, peer), device_id_type=MESH)
        return carry

    lax.fori_loop(1, T, greet_tile, 0)

    def greet_state(step, carry):
        peer = lax.rem(state + step, S)
        for index in range(4):
            pl.semaphore_signal(
                barrier, inc=1, device_id=(peer, 4 * index + swap(band)), device_id_type=MESH
            )
        return carry

    lax.fori_loop(1, S, greet_state, 0)

    loads = []
    for index, (source, target) in enumerate(
        [
            (gain, m.gain_v),
            (lbias, m.lbias_v),
            (wq, m.wq_v),
            (wk, m.wk_v),
            (wv, m.wv_v),
            (wg, m.wg_v),
            (wo, m.wo_v),
            (wpb, m.wpb_v),
            (gbias, m.gbias_v),
            (obias, m.obias_v),
            (wd, m.wd_v),
            (dbias, m.dbias_v),
            (targets.at[0, 0], m.targets_v),
            (tiles.at[0, 0], m.tile_v),
            (offsets, m.offsets_s),
        ]
    ):
        load = pltpu.make_async_copy(source, target, m.w_sem.at[index])
        load.start()
        loads.append(load)

    rows_i = lax.broadcasted_iota(I32, (C, C), 0)
    cols_i = lax.broadcasted_iota(I32, (C, C), 1)
    m.eye[...] = jnp.where(rows_i == cols_i, 1.0, 0.0).astype(BF16)
    for head in range(H):
        m.hmask[head] = jnp.where(cols_i // HD == head, 1.0, 0.0).astype(BF16)
    early = (0, 1, 7, 13)
    late_loads = [load for index, load in enumerate(loads) if index not in early]
    for index in early:
        loads[index].wait()
    eye = m.eye[...]
    m.gain_b[...] = column(m.gain_v[...])
    m.lbias_b[...] = column(m.lbias_v[...])
    for head in range(H):
        m.wpb_b[head] = column(m.wpb_v[head : head + 1])

    for index in range(R):
        z = dot_nt(eye, m.tile_v[4 * index : 4 * (index + 1)].reshape(L, C))
        centre = z - total(z) * (1.0 / C)
        inverse = lax.rsqrt(total(centre * centre) * (1.0 / C) + 1e-05)
        zn = centre * inverse * m.gain_b[...] + m.lbias_b[...]
        for head in range(H):
            m.b_rows[R * head + index : R * head + index + 1, :] = total(zn * m.wpb_b[head]) * LOG2E
    turned = jnp.transpose(m.b_rows[...])
    rows_s = lax.broadcasted_iota(I32, (32, L), 0)
    cols_s = lax.broadcasted_iota(I32, (32, L), 1)
    tile_bias = jnp.zeros((32, L), F32)
    for part in range(3):
        piece = turned.astype(BF16)
        turned = turned - piece.astype(F32)
        for index in range(4):
            lane = 32 * (rows_s // R) + 4 * (rows_s % R) + index
            place_it = jnp.where(lane == cols_s, 1.0, 0.0).astype(BF16)
            tile_bias = tile_bias + dot(piece[32 * index : 32 * (index + 1)], place_it)
    m.b_stage[...] = tile_bias

    pl.semaphore_wait(barrier, T - 1 + 4 * (S - 1))

    def tile_copy(step):
        other = lax.rem(sub + step, 4)
        return pltpu.make_async_remote_copy(
            src_ref=tiles.at[0, 0, pl.ds(R * swap(other), R)],
            dst_ref=m.zb.at[:, pl.ds(pl.multiple_of(32 * sub, 32), 32), :],
            send_sem=m.a_send.at[step],
            recv_sem=m.a_sem,
            device_id=(state, 4 * band + other),
            device_id_type=MESH,
        )

    half = tile // 8
    place = tile % 8
    partner = 8 * (1 - half) + place

    def bias_copy(source, slot, index, sem, dest):
        return pltpu.make_async_remote_copy(
            src_ref=source,
            dst_ref=m.b_recv.at[slot],
            send_sem=m.b_send.at[index],
            recv_sem=m.b_sem.at[sem],
            device_id=(state, dest),
            device_id_type=MESH,
        )

    bias_copy(m.b_stage, tile, 0, 0, partner).start()
    for step in (2, 3, 1):
        tile_copy(step).start()
    pltpu.make_async_copy(
        tiles.at[0, 0, pl.ds(R * group, R)],
        m.zb.at[:, pl.ds(pl.multiple_of(32 * sub, 32), 32), :],
        m.a_sem,
    ).start()
    for step in range(1, 8):
        dest = 8 * half + (place + step) % 8
        bias_copy(m.b_stage, tile, step, 1, dest).start()
    pltpu.make_async_copy(m.b_stage, m.b_recv.at[tile], m.b_sem.at[1]).start()

    for load in late_loads:
        load.wait()
    m.shift[...] = jnp.where(((rows_i - m.offsets_s[state] + L) & (L - 1)) == cols_i, 1.0, 0.0).astype(BF16)
    rows_o = lax.broadcasted_iota(I32, (256, L), 0)
    cols_o = lax.broadcasted_iota(I32, (256, L), 1)
    row_in = 8 * ((rows_o >> 4) & 1) + (rows_o & 7)
    same_row = row_in == (cols_o & 15)
    band_gap = 32 * ((rows_o >> 5) - ((cols_o >> 4) & 3))
    upper_half = (rows_o >> 3) & 1
    for index in range(S // 2):
        offset = jnp.where(cols_o < 64, m.offsets_s[2 * index], m.offsets_s[2 * index + 1])
        wrapped = jnp.where(offset > 8 * state, 1, 0)
        chosen = same_row & (band_gap == offset) & (upper_half == wrapped)
        m.spread[:, L * index : L * (index + 1)] = jnp.where(chosen, 1.0, 0.0).astype(BF16)
    for index in range(4):
        m.tg_stage[index] = jnp.concatenate([m.targets_v[:, index, :]] * 4, axis=0)
    for index in range(4):
        dest = 4 * index + swap(band)

        @pl.when(dest != tile)
        def _():
            pltpu.make_async_remote_copy(
                src_ref=m.tg_stage.at[index],
                dst_ref=m.tg_recv.at[sub],
                send_sem=m.tg_send.at[index],
                recv_sem=m.tg_sem,
                device_id=(state, dest),
                device_id_type=MESH,
            ).start()

        @pl.when(dest == tile)
        def _():
            pltpu.make_async_copy(m.tg_stage.at[index], m.tg_recv.at[sub], m.tg_sem).start()

    for index, ref in enumerate((m.wq_v, m.wk_v, m.wv_v, m.wg_v)):
        weight = ref[...]
        m.w_in[:, C * index : C * (index + 1)] = weight
        m.w_in_t[C * index : C * (index + 1), :] = dot_nt(eye, weight).astype(BF16)
    m.wo_t[...] = dot_nt(eye, m.wo_v[...]).astype(BF16)
    head_w = m.wd_v[...]
    high, low = halves(2.0 * jnp.transpose(head_w))
    m.wd3[...] = jnp.concatenate([high, high, low], axis=1)
    high, low = halves(head_w - total(head_w) * (1.0 / NB))
    m.wd_t3[...] = jnp.concatenate([high, high, low], axis=1)
    m.gbias_b[...] = column(m.gbias_v[...])
    m.obias_b[...] = column(m.obias_v[...])
    m.dbias_b[...] = column(m.dbias_v[...])

    pltpu.make_async_copy(m.zb, m.zb, m.a_sem).wait()

    def norm_row(row, carry):
        z = dot_nt(m.eye[...], m.zb[row])
        centre = z - total(z) * (1.0 / C)
        inverse = lax.rsqrt(total(centre * centre) * (1.0 / C) + 1e-05)
        normed = centre * inverse
        zn = normed * m.gain_b[...] + m.lbias_b[...]
        m.zt[row] = z
        m.xh[row] = normed
        m.inv[row] = inverse
        m.znb[row] = zn.astype(BF16)
        return carry

    lax.fori_loop(0, R, norm_row, 0, unroll=True)

    pltpu.make_async_copy(m.b_stage, m.b_recv.at[partner], m.b_sem.at[0]).wait()
    for step in range(1, 8):
        dest = 8 * half + (place + step) % 8
        bias_copy(m.b_recv.at[partner], partner, 7 + step, 2, dest).start()

    for row in range(0, R, 2):
        proj = dot(m.w_in_t[...], jnp.concatenate([m.znb[row], m.znb[row + 1]], axis=1))
        queries_keys_values = proj[: 3 * C].astype(BF16)
        gates = proj[3 * C :]
        for side in range(2):
            here = row + side
            span = slice(L * side, L * (side + 1))
            m.qt[here] = queries_keys_values[:C, span]
            m.kt[here] = queries_keys_values[C : 2 * C, span]
            m.vt[here] = queries_keys_values[2 * C :, span]
            m.gt[here] = jax.nn.sigmoid(gates[:, span] + m.gbias_b[...])
            natural = dot_nt(m.eye[...], queries_keys_values[C:, span]).astype(BF16)
            m.vn[here] = natural[:, C:]
            stacked = jnp.concatenate([natural[:, :C] * m.hmask[head] for head in range(H)], axis=0)
            scores = dot(stacked, queries_keys_values[:C, span]) * (INV_ROOT * LOG2E)
            m.at[here] = scores.reshape(H, L, L)

    pltpu.make_async_copy(m.b_recv.at[pl.ds(0, 8)], m.b_recv.at[pl.ds(0, 8)], m.b_sem.at[1]).wait()
    pltpu.make_async_copy(m.b_recv.at[pl.ds(0, 7)], m.b_recv.at[pl.ds(0, 7)], m.b_sem.at[2]).wait()
    bands = [m.b_recv[4 * index : 4 * (index + 1)].reshape(L, L) for index in range(4)]
    for head in range(H):
        m.bias_t[head] = jnp.concatenate([part[:, 32 * head : 32 * (head + 1)] for part in bands], axis=1)

    def attend(row):
        values = m.vt[row]
        parts = []
        for head in range(H):
            scores = m.at[row, head] + m.bias_t[head]
            top = jnp.max(scores, axis=0, keepdims=True)
            weights = jnp.exp2(scores - top)
            weights = weights * (1.0 / total(weights))
            m.at[row, head] = weights
            parts.append(dot(values[HD * head : HD * (head + 1)], weights.astype(BF16)))
        attended = jnp.concatenate(parts, axis=0)
        m.ot[row] = attended
        return (m.gt[row] * attended).astype(BF16)

    def predict(row, gated):
        added = dot(m.wo_t[...], jnp.concatenate(gated, axis=1))
        updated = jnp.concatenate([m.zt[row] + m.obias_b[...], m.zt[row + 1] + m.obias_b[...]], axis=1) + added
        logits = dot(m.wd_t3[...], three(updated))
        m.lgt[row] = logits[:, :L]
        m.lgt[row + 1] = logits[:, L:]
        rounded = logits.astype(BF16)
        first, second = rounded[:, :L], rounded[:, L:]
        turned = dot_nt(m.eye[...], jnp.concatenate([first, first, second, second], axis=0))
        m.lgn[L * row : L * (row + 1), :] = turned[:, :C]
        m.lgn[L * (row + 1) : L * (row + 2), :] = turned[:, C:]

    waiting = None
    for row in range(0, R, 2):
        gated = [attend(row), attend(row + 1)]
        if waiting is not None:
            predict(*waiting)
        waiting = (row, gated)
    predict(*waiting)

    order = [(1, d) for d in (4, 3, 5, 2, 6, 1, 7, 0)] + [(0, d) for d in (4, 3, 5, 2, 6, 1, 7, 0)]

    def peer_of(flip, step):
        return 8 * (half + flip * (1 - 2 * half)) + (place + step) % 8

    low_lanes = lax.broadcasted_iota(I32, (8, L), 1) < NB

    for index, (flip, step) in enumerate(order):
        dest = peer_of(flip, step)
        theirs = block_of(dest)
        parts = []
        for column_in in range(4):
            first = m.lgn[pl.ds(8 * theirs + column_in, 8, stride=L), :]
            second = m.lgn[pl.ds(8 * theirs + 4 + column_in, 8, stride=L), :]
            parts.append(jnp.where(low_lanes, first, second))
        m.c_stage[theirs] = jnp.concatenate(parts, axis=0).astype(BF16)
        if index < T - 1:
            pltpu.make_async_remote_copy(
                src_ref=m.c_stage.at[theirs],
                dst_ref=m.c_recv.at[block],
                send_sem=m.c_send.at[index],
                recv_sem=m.c_sem,
                device_id=(state, dest),
                device_id_type=MESH,
            ).start()
        else:
            pltpu.make_async_copy(m.c_stage.at[block], m.c_recv.at[block], m.c_sem).start()

    pltpu.make_async_copy(m.tg_recv, m.tg_recv, m.tg_sem).wait()
    pltpu.make_async_copy(m.c_recv, m.c_recv, m.c_sem).wait()

    received = [m.c_recv[peer].astype(F32) for peer in range(T)]
    for index in range(4):
        rows = jnp.concatenate([block[8 * index : 8 * (index + 1)] for block in received], axis=0)
        turned = jnp.transpose(rows)
        m.mirror[index] = turned[:NB]
        m.mirror[4 + index] = turned[NB:]

    bins = lax.broadcasted_iota(I32, (NB, L), 0)

    def residual(row):
        logits = m.lgt[row] + m.mirror[row] + m.dbias_b[...]
        top = jnp.max(logits, axis=0, keepdims=True)
        expo = jnp.exp(logits - top)
        prob = expo * (1.0 / total(expo))
        wanted = m.tg_recv[row // 2, row % 2 : row % 2 + 1, :]
        return prob - jnp.where(bins == wanted, 1.0, 0.0)

    def out_gradient(row):
        pair_grad = dot(m.wd3[...], three(jnp.concatenate([residual(row), residual(row + 1)], axis=1)))
        m.dp[row] = pair_grad[:, :L]
        m.dp[row + 1] = pair_grad[:, L:]
        return dot(m.wo_v[...], pair_grad.astype(BF16))

    def score_gradients(row, out_grad):
        weight_grads = []
        for side in range(2):
            here = row + side
            gate = m.gt[here]
            gated = out_grad[:, L * side : L * (side + 1)] * gate
            att_grad = gated.astype(BF16)
            m.dot[here] = att_grad
            m.dgt[here] = (gated * m.ot[here] * (1.0 - gate)).astype(BF16)
            values_n = m.vn[here]
            stacked = jnp.concatenate([values_n * m.hmask[head] for head in range(H)], axis=0)
            weight_grads.append(dot(stacked, att_grad))
        for head in range(H):
            scores = []
            for side in range(2):
                weights = m.at[row + side, head]
                grads = weight_grads[side][L * head : L * (head + 1)]
                score = weights * (grads - total(weights * grads))
                m.score_b[row + side, head] = score.astype(BF16)
                scores.append(score)
            both = scores[0] + scores[1]
            m.dbt[head] = both if row == 0 else m.dbt[head] + both

    grads = out_gradient(0)
    for row in range(0, R, 2):
        current = grads
        if row + 2 < R:
            grads = out_gradient(row + 2)
        score_gradients(row, current)

    turned = [jnp.transpose(m.dbt[head]) for head in range(H)]
    for peer in range(T):
        m.e_stage[peer] = jnp.concatenate(
            [block[R * peer : R * (peer + 1)] for block in turned], axis=0
        ).astype(BF16)

    for index, (flip, step) in enumerate(order[:-1]):
        dest = peer_of(flip, step)
        pltpu.make_async_remote_copy(
            src_ref=m.e_stage.at[block_of(dest)],
            dst_ref=m.e_recv.at[block],
            send_sem=m.e_send.at[index],
            recv_sem=m.e_sem,
            device_id=(state, dest),
            device_id_type=MESH,
        ).start()
    pltpu.make_async_copy(m.e_stage.at[block], m.e_recv.at[block], m.e_sem).start()

    def projections(row):
        queries = m.qt[row]
        keys = m.kt[row]
        att_grad = m.dot[row]
        spans = [slice(HD * head, HD * (head + 1)) for head in range(H)]
        scores = [m.score_b[row, head] for head in range(H)]
        parts = [dot(keys[span], score) * INV_ROOT for span, score in zip(spans, scores)]
        parts += [dot_nt(queries[span], score) * INV_ROOT for span, score in zip(spans, scores)]
        parts += [dot_nt(att_grad[span], m.at[row, head].astype(BF16)) for head, span in enumerate(spans)]
        return jnp.concatenate([jnp.concatenate(parts, axis=0).astype(BF16), m.dgt[row]], axis=0)

    for row in range(0, R, 2):
        both = dot(m.w_in[...], jnp.concatenate([projections(row), projections(row + 1)], axis=1))
        m.zt[row] = both[:, :L]
        m.zt[row + 1] = both[:, L:]

    pltpu.make_async_copy(m.e_recv, m.e_recv, m.e_sem).wait()
    bias_sum = m.e_recv[0].astype(F32)
    for peer in range(1, T):
        bias_sum = bias_sum + m.e_recv[peer].astype(F32)
    m.dbs[...] = bias_sum

    def finish_pair(pair, carry):
        for side in range(2):
            row = 2 * pair + side
            zn_grad = m.zt[row]
            for head in range(H):
                zn_grad = zn_grad + m.wpb_b[head] * m.dbs[pl.ds(R * head + row, 1), :]
            scaled = zn_grad * m.gain_b[...]
            normed = m.xh[row]
            mean = total(scaled) * (1.0 / C)
            slope = total(scaled * normed) * (1.0 / C)
            result = m.dp[row] + m.inv[row] * (scaled - mean - normed * slope)
            m.grad[row] = dot_nt(m.shift[...], result.astype(BF16))

        target = 4 * group + pair
        for step, (dy, dz) in enumerate(state_order):
            dest = 4 * lax.rem(state // 4 + dy, 4) + lax.rem(state % 4 + dz, 4)
            start = pl.multiple_of(8 * dest, 8)
            upper = m.grad[2 * pair, pl.ds(start, 8), :]
            lower = m.grad[2 * pair + 1, pl.ds(start, 8), :]
            m.f_stage[pair, dest] = jnp.concatenate([upper, lower], axis=0).astype(BF16)

            def send(dest=dest, step=step):
                pltpu.make_async_remote_copy(
                    src_ref=m.f_stage.at[pair, dest],
                    dst_ref=m.f_recv.at[state, band],
                    send_sem=m.f_send.at[pair, step],
                    recv_sem=m.f_sem,
                    device_id=(dest, target),
                    device_id_type=MESH,
                ).start()

            if step < S - 1:
                send()
            else:
                pl.when(target != tile)(send)

                @pl.when(target == tile)
                def _():
                    pltpu.make_async_copy(
                        m.f_stage.at[pair, state], m.f_recv.at[state, band], m.f_sem
                    ).start()

        return carry

    state_order = [(dy, dz) for dy in (2, 1, 3, 0) for dz in (2, 1, 3, 0)]
    lax.fori_loop(0, 4, finish_pair, 0, unroll=True)

    for step in (2, 3, 1):
        tile_copy(step).wait_send()
    for index in range(4):

        @pl.when(4 * index + swap(band) != tile)
        def _():
            pltpu.make_async_copy(m.tg_stage.at[0], m.tg_stage.at[0], m.tg_send.at[index]).wait()

    for index in range(15):
        pltpu.make_async_copy(m.b_stage, m.b_stage, m.b_send.at[index]).wait()

    def sent(step, carry):
        pltpu.make_async_copy(m.c_stage.at[0], m.c_stage.at[0], m.c_send.at[step]).wait()
        pltpu.make_async_copy(m.e_stage.at[0], m.e_stage.at[0], m.e_send.at[step]).wait()
        return carry

    lax.fori_loop(0, T - 1, sent, 0)

    pltpu.make_async_copy(m.f_recv, m.f_recv, m.f_sem).wait()
    out[...] = dot(m.spread[...], m.f_recv[...].reshape(S * 64, C)).reshape(out.shape)

    def sent_state(step, carry):
        for pair in range(4):

            @pl.when(jnp.logical_or(step < S - 1, 4 * group + pair != tile))
            def _():
                pltpu.make_async_copy(
                    m.f_stage.at[0, 0], m.f_stage.at[0, 0], m.f_send.at[pair, step]
                ).wait()

        return carry

    lax.fori_loop(0, S, sent_state, 0)


def on_device(
    pair_tiles,
    targets,
    offsets,
    ln_gain,
    ln_bias,
    w_query,
    w_key,
    w_value,
    w_pairbias,
    w_gate,
    gate_bias,
    w_output,
    out_bias,
    w_distogram,
    dist_bias,
):
    anywhere = pl.BlockSpec(memory_space=pltpu.HBM)
    in_specs = [anywhere] * 15
    call = pl.pallas_call(
        kernel,
        out_shape=jax.ShapeDtypeStruct((8, 1, 2, 2, L // S, C), F32),
        in_specs=in_specs,
        out_specs=pl.BlockSpec(memory_space=pltpu.VMEM),
        scratch_shapes=list(SCRATCH.values()),
        compiler_params=pltpu.CompilerParams(
            collective_id=0, has_side_effects=True, vmem_limit_bytes=52 * 1024 * 1024
        ),
    )
    operands = (
        pair_tiles,
        targets,
        offsets,
        ln_gain.reshape(1, C),
        ln_bias.reshape(1, C),
        w_query,
        w_key,
        w_value,
        w_pairbias.T,
        w_gate,
        gate_bias.reshape(1, C),
        w_output,
        out_bias.reshape(1, C),
        w_distogram.T,
        dist_bias.reshape(1, NB),
    )
    operands = [
        pltpu.with_memory_space_constraint(operand, pltpu.HBM) for operand in operands
    ]
    return call(*operands)


def solution(mesh):
    in_specs = (
        P("state", "tile", None, None, None),
        P("state", "tile", None, None, None),
    ) + (P(),) * 13
    out_specs = P(None, "tile", None, None, "state", None)
    return jax.shard_map(
        on_device, mesh=mesh, in_specs=in_specs, out_specs=out_specs, check_vma=False
    )
```

```python
import math

import jax
import jax.numpy as jnp
from jax import lax
from jax.experimental import pallas as pl
from jax.experimental.pallas import tpu as pltpu
from jax.sharding import PartitionSpec as P

C = 128
H = 4
HD = 32
NB = 64
L = 128
S = 16
T = 16
R = 8
F32 = jnp.float32
BF16 = jnp.bfloat16
I32 = jnp.int32
MESH = pl.DeviceIdType.MESH
LOG2E = 1.0 / math.log(2.0)
INV_ROOT = 1.0 / math.sqrt(HD)

SCRATCH = dict(
    gain_v=pltpu.VMEM((1, C), F32),
    lbias_v=pltpu.VMEM((1, C), F32),
    wq_v=pltpu.VMEM((C, C), BF16),
    wk_v=pltpu.VMEM((C, C), BF16),
    wv_v=pltpu.VMEM((C, C), BF16),
    wg_v=pltpu.VMEM((C, C), BF16),
    wo_v=pltpu.VMEM((C, C), BF16),
    wpb_v=pltpu.VMEM((H, C), F32),
    gbias_v=pltpu.VMEM((1, C), F32),
    obias_v=pltpu.VMEM((1, C), F32),
    wd_v=pltpu.VMEM((NB, C), F32),
    dbias_v=pltpu.VMEM((1, NB), F32),
    targets_v=pltpu.VMEM((2, 4, L), I32),
    offsets_s=pltpu.SMEM((S,), I32),
    w_sem=pltpu.SemaphoreType.DMA((15,)),
    eye=pltpu.VMEM((C, C), BF16),
    hmask=pltpu.VMEM((H, C, C), BF16),
    shift=pltpu.VMEM((L, L), BF16),
    spread=pltpu.VMEM((256, S * 64), BF16),
    w_in_t=pltpu.VMEM((4 * C, C), BF16),
    w_in=pltpu.VMEM((C, 4 * C), BF16),
    wo_t=pltpu.VMEM((C, C), BF16),
    wd_t3=pltpu.VMEM((NB, 3 * C), BF16),
    wd3=pltpu.VMEM((C, 3 * NB), BF16),
    gain_b=pltpu.VMEM((C, L), F32),
    lbias_b=pltpu.VMEM((C, L), F32),
    gbias_b=pltpu.VMEM((C, L), F32),
    obias_b=pltpu.VMEM((C, L), F32),
    dbias_b=pltpu.VMEM((NB, L), F32),
    wpb_b=pltpu.VMEM((H, C, L), F32),
    zb=pltpu.VMEM((R, L, C), BF16),
    zt=pltpu.VMEM((R, C, L), F32),
    xh=pltpu.VMEM((R, C, L), F32),
    inv=pltpu.VMEM((R, 1, L), F32),
    znb=pltpu.VMEM((R, C, L), BF16),
    qt=pltpu.VMEM((R, C, L), BF16),
    kt=pltpu.VMEM((R, C, L), BF16),
    vt=pltpu.VMEM((R, C, L), BF16),
    vn=pltpu.VMEM((R, L, C), BF16),
    gt=pltpu.VMEM((R, C, L), F32),
    ot=pltpu.VMEM((R, C, L), F32),
    at=pltpu.VMEM((R, H, L, L), F32),
    bias_t=pltpu.VMEM((H, L, L), F32),
    lgt=pltpu.VMEM((R, NB, L), F32),
    lgn=pltpu.VMEM((R * L + L, C), F32),
    mirror=pltpu.VMEM((R, NB, L), F32),
    dp=pltpu.VMEM((R, C, L), F32),
    dgt=pltpu.VMEM((R, C, L), BF16),
    dot=pltpu.VMEM((R, C, L), BF16),
    score_b=pltpu.VMEM((R, H, L, L), BF16),
    dbt=pltpu.VMEM((H, L, L), F32),
    dbs=pltpu.VMEM((H * R, L), F32),
    grad=pltpu.VMEM((R, L, C), F32),
    tg_stage=pltpu.VMEM((4, 8, L), I32),
    tg_recv=pltpu.VMEM((4, 8, L), I32),
    tile_v=pltpu.VMEM((32, 32, C), BF16),
    b_rows=pltpu.VMEM((H * R, L), F32),
    b_stage=pltpu.VMEM((32, L), F32),
    b_recv=pltpu.VMEM((T, 32, L), F32),
    c_stage=pltpu.VMEM((T, 32, L), BF16),
    c_recv=pltpu.VMEM((T, 32, L), BF16),
    e_stage=pltpu.VMEM((T, 32, L), BF16),
    e_recv=pltpu.VMEM((T, 32, L), BF16),
    f_stage=pltpu.VMEM((4, S, 16, C), BF16),
    f_recv=pltpu.VMEM((S, 4, 16, C), BF16),
    a_send=pltpu.SemaphoreType.DMA((4,)),
    a_sem=pltpu.SemaphoreType.DMA,
    tg_send=pltpu.SemaphoreType.DMA((4,)),
    tg_sem=pltpu.SemaphoreType.DMA,
    b_send=pltpu.SemaphoreType.DMA((16,)),
    b_sem=pltpu.SemaphoreType.DMA((3,)),
    c_send=pltpu.SemaphoreType.DMA((T,)),
    c_sem=pltpu.SemaphoreType.DMA,
    e_send=pltpu.SemaphoreType.DMA((T,)),
    e_sem=pltpu.SemaphoreType.DMA,
    f_send=pltpu.SemaphoreType.DMA((4, S)),
    f_sem=pltpu.SemaphoreType.DMA,
)
NAMES = tuple(SCRATCH)


class Refs:
    pass


def dot(left, right):
    return jnp.dot(left, right, preferred_element_type=F32)


def dot_nt(left, right):
    return lax.dot_general(left, right, (((1,), (1,)), ((), ())), preferred_element_type=F32)


def halves(values):
    high = values.astype(BF16)
    low = (values - high.astype(F32)).astype(BF16)
    return high, low


def three(values):
    high, low = halves(values)
    return jnp.concatenate([high, low, high], axis=0)


def total(values):
    return jnp.sum(values, axis=0, keepdims=True)


def swap(index):
    return 2 * (index % 2) + index // 2


def block_of(device):
    return device - device % 4 + swap(device % 4)


def column(row):
    width = row.shape[1]
    return jnp.transpose(jnp.broadcast_to(row, (L, width)))


def kernel(
    tiles,
    targets,
    offsets,
    gain,
    lbias,
    wq,
    wk,
    wv,
    wpb,
    wg,
    gbias,
    wo,
    obias,
    wd,
    dbias,
    out,
    *scratch,
):
    m = Refs()
    for name, ref in zip(NAMES, scratch):
        setattr(m, name, ref)
    state = lax.axis_index("state")
    tile = lax.axis_index("tile")
    band = tile // 4
    sub = tile % 4
    group = swap(sub)
    block = 4 * band + group

    barrier = pltpu.get_barrier_semaphore()

    def greet_tile(step, carry):
        peer = lax.rem(tile + step, T)
        pl.semaphore_signal(barrier, inc=1, device_id=(state, peer), device_id_type=MESH)
        return carry

    lax.fori_loop(1, T, greet_tile, 0)

    def greet_state(step, carry):
        peer = lax.rem(state + step, S)
        for index in range(4):
            pl.semaphore_signal(
                barrier, inc=1, device_id=(peer, 4 * index + swap(band)), device_id_type=MESH
            )
        return carry

    lax.fori_loop(1, S, greet_state, 0)

    loads = []
    for index, (source, target) in enumerate(
        [
            (gain, m.gain_v),
            (lbias, m.lbias_v),
            (wq, m.wq_v),
            (wk, m.wk_v),
            (wv, m.wv_v),
            (wg, m.wg_v),
            (wo, m.wo_v),
            (wpb, m.wpb_v),
            (gbias, m.gbias_v),
            (obias, m.obias_v),
            (wd, m.wd_v),
            (dbias, m.dbias_v),
            (targets.at[0, 0], m.targets_v),
            (tiles.at[0, 0], m.tile_v),
            (offsets, m.offsets_s),
        ]
    ):
        load = pltpu.make_async_copy(source, target, m.w_sem.at[index])
        load.start()
        loads.append(load)

    rows_i = lax.broadcasted_iota(I32, (C, C), 0)
    cols_i = lax.broadcasted_iota(I32, (C, C), 1)
    m.eye[...] = jnp.where(rows_i == cols_i, 1.0, 0.0).astype(BF16)
    for head in range(H):
        m.hmask[head] = jnp.where(cols_i // HD == head, 1.0, 0.0).astype(BF16)
    early = (0, 1, 7, 13)
    late_loads = [load for index, load in enumerate(loads) if index not in early]
    for index in early:
        loads[index].wait()
    eye = m.eye[...]
    m.gain_b[...] = column(m.gain_v[...])
    m.lbias_b[...] = column(m.lbias_v[...])
    for head in range(H):
        m.wpb_b[head] = column(m.wpb_v[head : head + 1])

    for index in range(R):
        z = dot_nt(eye, m.tile_v[4 * index : 4 * (index + 1)].reshape(L, C))
        centre = z - total(z) * (1.0 / C)
        inverse = lax.rsqrt(total(centre * centre) * (1.0 / C) + 1e-05)
        zn = centre * inverse * m.gain_b[...] + m.lbias_b[...]
        for head in range(H):
            m.b_rows[R * head + index : R * head + index + 1, :] = total(zn * m.wpb_b[head]) * LOG2E
    turned = jnp.transpose(m.b_rows[...])
    rows_s = lax.broadcasted_iota(I32, (32, L), 0)
    cols_s = lax.broadcasted_iota(I32, (32, L), 1)
    tile_bias = jnp.zeros((32, L), F32)
    for part in range(3):
        piece = turned.astype(BF16)
        turned = turned - piece.astype(F32)
        for index in range(4):
            lane = 32 * (rows_s // R) + 4 * (rows_s % R) + index
            place_it = jnp.where(lane == cols_s, 1.0, 0.0).astype(BF16)
            tile_bias = tile_bias + dot(piece[32 * index : 32 * (index + 1)], place_it)
    m.b_stage[...] = tile_bias

    pl.semaphore_wait(barrier, T - 1 + 4 * (S - 1))

    def tile_copy(step):
        other = lax.rem(sub + step, 4)
        return pltpu.make_async_remote_copy(
            src_ref=tiles.at[0, 0, pl.ds(R * swap(other), R)],
            dst_ref=m.zb.at[:, pl.ds(pl.multiple_of(32 * sub, 32), 32), :],
            send_sem=m.a_send.at[step],
            recv_sem=m.a_sem,
            device_id=(state, 4 * band + other),
            device_id_type=MESH,
        )

    half = tile // 8
    place = tile % 8
    partner = 8 * (1 - half) + place

    def bias_copy(source, slot, index, sem, dest):
        return pltpu.make_async_remote_copy(
            src_ref=source,
            dst_ref=m.b_recv.at[slot],
            send_sem=m.b_send.at[index],
            recv_sem=m.b_sem.at[sem],
            device_id=(state, dest),
            device_id_type=MESH,
        )

    bias_copy(m.b_stage, tile, 0, 0, partner).start()
    for step in (2, 3, 1):
        tile_copy(step).start()
    pltpu.make_async_copy(
        tiles.at[0, 0, pl.ds(R * group, R)],
        m.zb.at[:, pl.ds(pl.multiple_of(32 * sub, 32), 32), :],
        m.a_sem,
    ).start()
    for step in range(1, 8):
        dest = 8 * half + (place + step) % 8
        bias_copy(m.b_stage, tile, step, 1, dest).start()
    pltpu.make_async_copy(m.b_stage, m.b_recv.at[tile], m.b_sem.at[1]).start()

    for load in late_loads:
        load.wait()
    m.shift[...] = jnp.where(((rows_i - m.offsets_s[state] + L) & (L - 1)) == cols_i, 1.0, 0.0).astype(BF16)
    rows_o = lax.broadcasted_iota(I32, (256, L), 0)
    cols_o = lax.broadcasted_iota(I32, (256, L), 1)
    row_in = 8 * ((rows_o >> 4) & 1) + (rows_o & 7)
    same_row = row_in == (cols_o & 15)
    band_gap = 32 * ((rows_o >> 5) - ((cols_o >> 4) & 3))
    upper_half = (rows_o >> 3) & 1
    for index in range(S // 2):
        offset = jnp.where(cols_o < 64, m.offsets_s[2 * index], m.offsets_s[2 * index + 1])
        wrapped = jnp.where(offset > 8 * state, 1, 0)
        chosen = same_row & (band_gap == offset) & (upper_half == wrapped)
        m.spread[:, L * index : L * (index + 1)] = jnp.where(chosen, 1.0, 0.0).astype(BF16)
    for index in range(4):
        m.tg_stage[index] = jnp.concatenate([m.targets_v[:, index, :]] * 4, axis=0)
    for index in range(4):
        dest = 4 * index + swap(band)

        @pl.when(dest != tile)
        def _():
            pltpu.make_async_remote_copy(
                src_ref=m.tg_stage.at[index],
                dst_ref=m.tg_recv.at[sub],
                send_sem=m.tg_send.at[index],
                recv_sem=m.tg_sem,
                device_id=(state, dest),
                device_id_type=MESH,
            ).start()

        @pl.when(dest == tile)
        def _():
            pltpu.make_async_copy(m.tg_stage.at[index], m.tg_recv.at[sub], m.tg_sem).start()

    for index, ref in enumerate((m.wq_v, m.wk_v, m.wv_v, m.wg_v)):
        weight = ref[...]
        m.w_in[:, C * index : C * (index + 1)] = weight
        m.w_in_t[C * index : C * (index + 1), :] = dot_nt(eye, weight).astype(BF16)
    m.wo_t[...] = dot_nt(eye, m.wo_v[...]).astype(BF16)
    head_w = m.wd_v[...]
    high, low = halves(2.0 * jnp.transpose(head_w))
    m.wd3[...] = jnp.concatenate([high, high, low], axis=1)
    high, low = halves(head_w - total(head_w) * (1.0 / NB))
    m.wd_t3[...] = jnp.concatenate([high, high, low], axis=1)
    m.gbias_b[...] = column(m.gbias_v[...])
    m.obias_b[...] = column(m.obias_v[...])
    m.dbias_b[...] = column(m.dbias_v[...])

    pltpu.make_async_copy(m.zb, m.zb, m.a_sem).wait()

    def norm_row(row, carry):
        z = dot_nt(m.eye[...], m.zb[row])
        centre = z - total(z) * (1.0 / C)
        inverse = lax.rsqrt(total(centre * centre) * (1.0 / C) + 1e-05)
        normed = centre * inverse
        zn = normed * m.gain_b[...] + m.lbias_b[...]
        m.zt[row] = z
        m.xh[row] = normed
        m.inv[row] = inverse
        m.znb[row] = zn.astype(BF16)
        return carry

    lax.fori_loop(0, R, norm_row, 0, unroll=True)

    pltpu.make_async_copy(m.b_stage, m.b_recv.at[partner], m.b_sem.at[0]).wait()
    for step in range(1, 8):
        dest = 8 * half + (place + step) % 8
        bias_copy(m.b_recv.at[partner], partner, 7 + step, 2, dest).start()

    for row in range(0, R, 2):
        proj = dot(m.w_in_t[...], jnp.concatenate([m.znb[row], m.znb[row + 1]], axis=1))
        queries_keys_values = proj[: 3 * C].astype(BF16)
        gates = proj[3 * C :]
        for side in range(2):
            here = row + side
            span = slice(L * side, L * (side + 1))
            m.qt[here] = queries_keys_values[:C, span]
            m.kt[here] = queries_keys_values[C : 2 * C, span]
            m.vt[here] = queries_keys_values[2 * C :, span]
            m.gt[here] = jax.nn.sigmoid(gates[:, span] + m.gbias_b[...])
            natural = dot_nt(m.eye[...], queries_keys_values[C:, span]).astype(BF16)
            m.vn[here] = natural[:, C:]
            stacked = jnp.concatenate([natural[:, :C] * m.hmask[head] for head in range(H)], axis=0)
            scores = dot(stacked, queries_keys_values[:C, span]) * (INV_ROOT * LOG2E)
            m.at[here] = scores.reshape(H, L, L)

    pltpu.make_async_copy(m.b_recv.at[pl.ds(0, 8)], m.b_recv.at[pl.ds(0, 8)], m.b_sem.at[1]).wait()
    pltpu.make_async_copy(m.b_recv.at[pl.ds(0, 7)], m.b_recv.at[pl.ds(0, 7)], m.b_sem.at[2]).wait()
    bands = [m.b_recv[4 * index : 4 * (index + 1)].reshape(L, L) for index in range(4)]
    for head in range(H):
        m.bias_t[head] = jnp.concatenate([part[:, 32 * head : 32 * (head + 1)] for part in bands], axis=1)

    def attend(row):
        values = m.vt[row]
        parts = []
        for head in range(H):
            scores = m.at[row, head] + m.bias_t[head]
            top = jnp.max(scores, axis=0, keepdims=True)
            weights = jnp.exp2(scores - top)
            weights = weights * (1.0 / total(weights))
            m.at[row, head] = weights
            parts.append(dot(values[HD * head : HD * (head + 1)], weights.astype(BF16)))
        attended = jnp.concatenate(parts, axis=0)
        m.ot[row] = attended
        return (m.gt[row] * attended).astype(BF16)

    def predict(row, gated):
        added = dot(m.wo_t[...], jnp.concatenate(gated, axis=1))
        updated = jnp.concatenate([m.zt[row] + m.obias_b[...], m.zt[row + 1] + m.obias_b[...]], axis=1) + added
        logits = dot(m.wd_t3[...], three(updated))
        m.lgt[row] = logits[:, :L]
        m.lgt[row + 1] = logits[:, L:]
        rounded = logits.astype(BF16)
        first, second = rounded[:, :L], rounded[:, L:]
        turned = dot_nt(m.eye[...], jnp.concatenate([first, first, second, second], axis=0))
        m.lgn[L * row : L * (row + 1), :] = turned[:, :C]
        m.lgn[L * (row + 1) : L * (row + 2), :] = turned[:, C:]

    waiting = None
    for row in range(0, R, 2):
        gated = [attend(row), attend(row + 1)]
        if waiting is not None:
            predict(*waiting)
        waiting = (row, gated)
    predict(*waiting)

    order = [(1, d) for d in (4, 3, 5, 2, 6, 1, 7, 0)] + [(0, d) for d in (4, 3, 5, 2, 6, 1, 7, 0)]

    def peer_of(flip, step):
        return 8 * (half + flip * (1 - 2 * half)) + (place + step) % 8

    low_lanes = lax.broadcasted_iota(I32, (8, L), 1) < NB

    for index, (flip, step) in enumerate(order):
        dest = peer_of(flip, step)
        theirs = block_of(dest)
        parts = []
        for column_in in range(4):
            first = m.lgn[pl.ds(8 * theirs + column_in, 8, stride=L), :]
            second = m.lgn[pl.ds(8 * theirs + 4 + column_in, 8, stride=L), :]
            parts.append(jnp.where(low_lanes, first, second))
        m.c_stage[theirs] = jnp.concatenate(parts, axis=0).astype(BF16)
        if index < T - 1:
            pltpu.make_async_remote_copy(
                src_ref=m.c_stage.at[theirs],
                dst_ref=m.c_recv.at[block],
                send_sem=m.c_send.at[index],
                recv_sem=m.c_sem,
                device_id=(state, dest),
                device_id_type=MESH,
            ).start()
        else:
            pltpu.make_async_copy(m.c_stage.at[block], m.c_recv.at[block], m.c_sem).start()

    pltpu.make_async_copy(m.tg_recv, m.tg_recv, m.tg_sem).wait()
    pltpu.make_async_copy(m.c_recv, m.c_recv, m.c_sem).wait()

    received = [m.c_recv[peer].astype(F32) for peer in range(T)]
    for index in range(4):
        rows = jnp.concatenate([block[8 * index : 8 * (index + 1)] for block in received], axis=0)
        turned = jnp.transpose(rows)
        m.mirror[index] = turned[:NB]
        m.mirror[4 + index] = turned[NB:]

    bins = lax.broadcasted_iota(I32, (NB, L), 0)

    def residual(row):
        logits = m.lgt[row] + m.mirror[row] + m.dbias_b[...]
        top = jnp.max(logits, axis=0, keepdims=True)
        expo = jnp.exp(logits - top)
        prob = expo * (1.0 / total(expo))
        wanted = m.tg_recv[row // 2, row % 2 : row % 2 + 1, :]
        return prob - jnp.where(bins == wanted, 1.0, 0.0)

    def out_gradient(row):
        pair_grad = dot(m.wd3[...], three(jnp.concatenate([residual(row), residual(row + 1)], axis=1)))
        m.dp[row] = pair_grad[:, :L]
        m.dp[row + 1] = pair_grad[:, L:]
        return dot(m.wo_v[...], pair_grad.astype(BF16))

    def score_gradients(row, out_grad):
        weight_grads = []
        for side in range(2):
            here = row + side
            gate = m.gt[here]
            gated = out_grad[:, L * side : L * (side + 1)] * gate
            att_grad = gated.astype(BF16)
            m.dot[here] = att_grad
            m.dgt[here] = (gated * m.ot[here] * (1.0 - gate)).astype(BF16)
            values_n = m.vn[here]
            stacked = jnp.concatenate([values_n * m.hmask[head] for head in range(H)], axis=0)
            weight_grads.append(dot(stacked, att_grad))
        for head in range(H):
            scores = []
            for side in range(2):
                weights = m.at[row + side, head]
                grads = weight_grads[side][L * head : L * (head + 1)]
                score = weights * (grads - total(weights * grads))
                m.score_b[row + side, head] = score.astype(BF16)
                scores.append(score)
            both = scores[0] + scores[1]
            m.dbt[head] = both if row == 0 else m.dbt[head] + both

    grads = out_gradient(0)
    for row in range(0, R, 2):
        current = grads
        if row + 2 < R:
            grads = out_gradient(row + 2)
        score_gradients(row, current)

    turned = [jnp.transpose(m.dbt[head]) for head in range(H)]
    for peer in range(T):
        m.e_stage[peer] = jnp.concatenate(
            [block[R * peer : R * (peer + 1)] for block in turned], axis=0
        ).astype(BF16)

    for index, (flip, step) in enumerate(order[:-1]):
        dest = peer_of(flip, step)
        pltpu.make_async_remote_copy(
            src_ref=m.e_stage.at[block_of(dest)],
            dst_ref=m.e_recv.at[block],
            send_sem=m.e_send.at[index],
            recv_sem=m.e_sem,
            device_id=(state, dest),
            device_id_type=MESH,
        ).start()
    pltpu.make_async_copy(m.e_stage.at[block], m.e_recv.at[block], m.e_sem).start()

    def projections(row):
        queries = m.qt[row]
        keys = m.kt[row]
        att_grad = m.dot[row]
        spans = [slice(HD * head, HD * (head + 1)) for head in range(H)]
        scores = [m.score_b[row, head] for head in range(H)]
        parts = [dot(keys[span], score) * INV_ROOT for span, score in zip(spans, scores)]
        parts += [dot_nt(queries[span], score) * INV_ROOT for span, score in zip(spans, scores)]
        parts += [dot_nt(att_grad[span], m.at[row, head].astype(BF16)) for head, span in enumerate(spans)]
        return jnp.concatenate([jnp.concatenate(parts, axis=0).astype(BF16), m.dgt[row]], axis=0)

    for row in range(0, R, 2):
        both = dot(m.w_in[...], jnp.concatenate([projections(row), projections(row + 1)], axis=1))
        m.zt[row] = both[:, :L]
        m.zt[row + 1] = both[:, L:]

    pltpu.make_async_copy(m.e_recv, m.e_recv, m.e_sem).wait()
    bias_sum = m.e_recv[0].astype(F32)
    for peer in range(1, T):
        bias_sum = bias_sum + m.e_recv[peer].astype(F32)
    m.dbs[...] = bias_sum

    def finish_pair(pair, carry):
        for side in range(2):
            row = 2 * pair + side
            zn_grad = m.zt[row]
            for head in range(H):
                zn_grad = zn_grad + m.wpb_b[head] * m.dbs[pl.ds(R * head + row, 1), :]
            scaled = zn_grad * m.gain_b[...]
            normed = m.xh[row]
            mean = total(scaled) * (1.0 / C)
            slope = total(scaled * normed) * (1.0 / C)
            result = m.dp[row] + m.inv[row] * (scaled - mean - normed * slope)
            m.grad[row] = dot_nt(m.shift[...], result.astype(BF16))

        target = 4 * group + pair
        for step, (dy, dz) in enumerate(state_order):
            dest = 4 * lax.rem(state // 4 + dy, 4) + lax.rem(state % 4 + dz, 4)
            start = pl.multiple_of(8 * dest, 8)
            upper = m.grad[2 * pair, pl.ds(start, 8), :]
            lower = m.grad[2 * pair + 1, pl.ds(start, 8), :]
            m.f_stage[pair, dest] = jnp.concatenate([upper, lower], axis=0).astype(BF16)

            def send(dest=dest, step=step):
                pltpu.make_async_remote_copy(
                    src_ref=m.f_stage.at[pair, dest],
                    dst_ref=m.f_recv.at[state, band],
                    send_sem=m.f_send.at[pair, step],
                    recv_sem=m.f_sem,
                    device_id=(dest, target),
                    device_id_type=MESH,
                ).start()

            if step < S - 1:
                send()
            else:
                pl.when(target != tile)(send)

                @pl.when(target == tile)
                def _():
                    pltpu.make_async_copy(
                        m.f_stage.at[pair, state], m.f_recv.at[state, band], m.f_sem
                    ).start()

        return carry

    state_order = [(dy, dz) for dy in (2, 1, 3, 0) for dz in (2, 1, 3, 0)]
    lax.fori_loop(0, 4, finish_pair, 0, unroll=True)

    for step in (2, 3, 1):
        tile_copy(step).wait_send()
    for index in range(4):

        @pl.when(4 * index + swap(band) != tile)
        def _():
            pltpu.make_async_copy(m.tg_stage.at[0], m.tg_stage.at[0], m.tg_send.at[index]).wait()

    for index in range(15):
        pltpu.make_async_copy(m.b_stage, m.b_stage, m.b_send.at[index]).wait()

    def sent(step, carry):
        pltpu.make_async_copy(m.c_stage.at[0], m.c_stage.at[0], m.c_send.at[step]).wait()
        pltpu.make_async_copy(m.e_stage.at[0], m.e_stage.at[0], m.e_send.at[step]).wait()
        return carry

    lax.fori_loop(0, T - 1, sent, 0)

    def sent_state(step, carry):
        for pair in range(4):

            @pl.when(jnp.logical_or(step < S - 1, 4 * group + pair != tile))
            def _():
                pltpu.make_async_copy(
                    m.f_stage.at[0, 0], m.f_stage.at[0, 0], m.f_send.at[pair, step]
                ).wait()

        return carry

    lax.fori_loop(0, S, sent_state, 0)

    pltpu.make_async_copy(m.f_recv, m.f_recv, m.f_sem).wait()
    out[...] = dot(m.spread[...], m.f_recv[...].reshape(S * 64, C)).reshape(out.shape)


def on_device(
    pair_tiles,
    targets,
    offsets,
    ln_gain,
    ln_bias,
    w_query,
    w_key,
    w_value,
    w_pairbias,
    w_gate,
    gate_bias,
    w_output,
    out_bias,
    w_distogram,
    dist_bias,
):
    anywhere = pl.BlockSpec(memory_space=pltpu.HBM)
    in_specs = [anywhere] * 15
    call = pl.pallas_call(
        kernel,
        out_shape=jax.ShapeDtypeStruct((8, 1, 2, 2, L // S, C), F32),
        in_specs=in_specs,
        out_specs=pl.BlockSpec(memory_space=pltpu.VMEM),
        scratch_shapes=list(SCRATCH.values()),
        compiler_params=pltpu.CompilerParams(
            collective_id=0, has_side_effects=True, vmem_limit_bytes=52 * 1024 * 1024
        ),
    )
    operands = (
        pair_tiles,
        targets,
        offsets,
        ln_gain.reshape(1, C),
        ln_bias.reshape(1, C),
        w_query,
        w_key,
        w_value,
        w_pairbias.T,
        w_gate,
        gate_bias.reshape(1, C),
        w_output,
        out_bias.reshape(1, C),
        w_distogram.T,
        dist_bias.reshape(1, NB),
    )
    operands = [
        pltpu.with_memory_space_constraint(operand, pltpu.HBM) for operand in operands
    ]
    return call(*operands)


def solution(mesh):
    in_specs = (
        P("state", "tile", None, None, None),
        P("state", "tile", None, None, None),
    ) + (P(),) * 13
    out_specs = P(None, "tile", None, None, "state", None)
    return jax.shard_map(
        on_device, mesh=mesh, in_specs=in_specs, out_specs=out_specs, check_vma=False
    )
```
